128 devices in a mesh: grp: 4 (over x), dev: 32 (over y, z, core).
Axes of the slice: x: 4, y: 4, z: 4, core: 2. Of those that a mesh axis runs over, the one named last changes fastest.
Arguments:
- query: bfloat16 [256, 8192], P(('grp', 'dev')), may hold values from -64 to 64
- key_cache: bfloat16 [256, 2048, 256], P(('grp', 'dev')), may hold values from -8 to 8
- value_cache: bfloat16 [256, 2048, 256], P(('grp', 'dev')), may hold values from -6 to 6
- lengths: int32 [256], P(('grp', 'dev')), may hold values from 0 to 2048, as said below
- hidden: bfloat16 [256, 7168], P(('grp', 'dev')), may hold values from -40 to 40
- out_weight: bfloat16 [8192, 7168], P(None, 'dev'), may hold values from -1 to 1
- ffn_gain: float32 [7168], replicated, may hold values from 0.1 to 1.9
- gate_weight: bfloat16 [7168, 16384], P(None, ('grp', 'dev')), may hold values from -0.0625 to 0.0625
- up_weight: bfloat16 [7168, 16384], P(None, ('grp', 'dev')), may hold values from -0.0625 to 0.0625
- down_weight: bfloat16 [7168, 16384], P(None, ('grp', 'dev')), may hold values from -0.1875 to 0.1875
Outputs:
- mixed: bfloat16 [256, 7168], P(('grp', 'dev'))
The draws below stay inside these ranges and needn't reach their ends.
Inputs may be any that keep to these rules, and one draw needn't show every extreme that they name: `lengths`: each slot holds 0 or 2 to 2048; the first slot holds 2048.
All inputs are finite; a program needn't handle non-finite values.
Results may differ from the reference program's by a relative error of at most 0.0075.
Values may be sent and summed in bfloat16 or wider, within the bound.
No kernel may reach another device: no remote copies, remote signals or barrier semaphores. Data moves between devices by JAX's collectives and lax.ppermute only.
A program may use at most 128 MiB of HBM per device.

```python
import math
import jax
import jax.numpy as jnp
from jax import lax

D = 7168
FF = 16384
HEADS = 32
HD = 256
LEN = 2048
ROWS = 256


def first_keys(key):
    return jnp.clip(jax.random.normal(key, (ROWS, HD), jnp.float32), -8.0, 8.0)


def draw_key_cache(key, part):
    shared = first_keys(key)
    key = jax.random.fold_in(key, 5)
    values = jnp.clip(jax.random.normal(key, (ROWS, LEN, HD), jnp.float32), -8.0, 8.0)
    values = values.at[:, 0, :].set(shared)
    return values.astype(jnp.bfloat16)


def draw_query(key, part):
    key = jax.random.fold_in(key, 7)
    values = jax.random.normal(key, (ROWS, HEADS, HD), jnp.float32)
    return jnp.clip(values, -64.0, 64.0).reshape(ROWS, HEADS * HD).astype(jnp.bfloat16)


def draw_lengths(key, part):
    key = jax.random.fold_in(key, 3)
    first_key, second_key, third_key = jax.random.split(key, 3)
    first = jax.random.randint(first_key, (ROWS,), 2, LEN + 1)
    second = jax.random.randint(second_key, (ROWS,), 2, LEN + 1)
    sizes = jnp.minimum(first, second)
    occupied = jax.random.randint(third_key, (ROWS,), 0, 4) > 0
    row_ids = jnp.arange(ROWS)
    sizes = jnp.where(occupied, sizes, 0)
    sizes = jnp.where(row_ids == 0, LEN, sizes)
    return sizes.astype(jnp.int32)


def draw_hidden(key, part):
    key = jax.random.fold_in(key, 11)
    first_key, second_key = jax.random.split(key, 2)
    base = jax.random.normal(first_key, (ROWS, D), jnp.float32)
    columns = jnp.exp(jax.random.uniform(second_key, (1, D), jnp.float32, 0.0, math.log(10.0))) / 3.0
    values = base * columns
    return jnp.clip(values, -40.0, 40.0).astype(jnp.bfloat16)


def raised(drawn, stream_key, source, target, parts, factor):
    def block_of(dim):
        return (jnp.arange(drawn.shape[dim]) // (drawn.shape[dim] // parts)).reshape((-1,) + (1,) * (drawn.ndim - 1 - dim))

    one_side = jax.random.permutation(stream_key, parts)[block_of(target)]
    far = (block_of(target) + parts // 2) % parts
    return jnp.where((block_of(source) == one_side) | (block_of(source) == far), factor * drawn, drawn)


def block_scale(key, shape, pieces, low, top_value):
    def one(axis_at, parts):
        steps = jax.random.uniform(jax.random.fold_in(jax.random.fold_in(key, 6), axis_at), (parts,), jnp.float32, low / len(pieces), top_value / len(pieces))
        return jnp.repeat(jnp.exp(steps), shape[axis_at] // parts).reshape((-1,) + (1,) * (len(shape) - axis_at - 1))

    loudness = one(*pieces[0])
    for cut in pieces[1:]:
        loudness = loudness * one(*cut)
    return loudness


def scatter_about(own_key, dims, width, most, cuts=(), held_as=jnp.bfloat16):
    gain = block_scale(own_key, dims, cuts, -0.22, 0.18) if cuts else 1.0
    values = jax.random.normal(own_key, dims, jnp.float32) * width * gain
    return jnp.minimum(jnp.maximum(values, -most), most).astype(held_as)


def heavy_noise(key, shape, width, most, cuts, heavy, kind=jnp.bfloat16):
    drawn = width * jax.random.normal(key, shape, jnp.float32)
    if cuts:
        drawn = drawn * block_scale(key, shape, cuts, -0.22, 0.18)
    return jnp.clip(raised(drawn, jax.random.fold_in(key, 3), *heavy), -most, most).astype(kind)


def setup_inputs(seed: int = 0) -> dict:
    key_of = jax.random.split(jax.random.key(seed), 11)
    return {
        "query": draw_query(jax.random.fold_in(key_of[10], 71), 0),
        "key_cache": draw_key_cache(jax.random.fold_in(key_of[10], 71), 0),
        "value_cache": scatter_about(key_of[2], (ROWS, LEN, HD), 1.0, 6.0, ((0, 128),)),
        "lengths": draw_lengths(jax.random.fold_in(key_of[10], 71), 0),
        "hidden": draw_hidden(jax.random.fold_in(key_of[10], 71), 0),
        "out_weight": scatter_about(key_of[5], (HEADS * HD, D), (max(1, HEADS * HD // 256)) ** -0.5, 1.0, ((1, 32),)),
        "ffn_gain": jnp.clip(1.0 + 0.18 * jax.random.normal(key_of[6], (D,), jnp.float32), 0.1, 1.9),
        "gate_weight": scatter_about(key_of[7], (D, FF), D ** -0.5, 0.0625, ((1, 128),)),
        "up_weight": scatter_about(key_of[8], (D, FF), D ** -0.5, 0.0625, ((1, 128),)),
        "down_weight": heavy_noise(key_of[9], (D, FF), FF ** -0.5, 0.1875, ((1, 128),), (1, 0, 128, 5.5)),
    }


def one_row(items):
    row_query, row_keys, row_values, row_length = items
    queries = row_query.reshape(HEADS, HD).astype(jnp.float32)
    scores = jnp.einsum('hd,td->ht', queries, row_keys.astype(jnp.float32)) * HD ** (-0.5)
    positions = lax.broadcasted_iota(jnp.int32, (1, LEN), 1)
    in_range = positions < jnp.maximum(row_length, 1)
    scores = jnp.where(in_range, scores, -jnp.inf)
    highest = lax.optimization_barrier(jnp.max(scores, axis=1, keepdims=True))
    weights = jnp.exp(scores - highest)
    probs = (weights / lax.optimization_barrier(jnp.sum(weights, axis=1, keepdims=True))).astype(jnp.bfloat16)
    attended = jnp.einsum('ht,td->hd', probs.astype(jnp.float32), row_values.astype(jnp.float32))
    return attended.reshape(HEADS * HD).astype(jnp.bfloat16)

def reference(query, key_cache, value_cache, lengths, hidden, out_weight, ffn_gain, gate_weight, up_weight, down_weight):
    attended = lax.map(one_row, (query, key_cache, value_cache, lengths))
    projected = jnp.dot(attended, out_weight, preferred_element_type=jnp.float32).astype(jnp.bfloat16)
    residual = hidden.astype(jnp.float32) + projected.astype(jnp.float32)
    scale = lax.rsqrt(lax.optimization_barrier(jnp.mean(residual * residual, axis=1, keepdims=True)) + 1e-05)
    normed = (residual * scale * ffn_gain).astype(jnp.bfloat16)
    gate_act = jnp.dot(normed, gate_weight, preferred_element_type=jnp.float32)
    up_act = jnp.dot(normed, up_weight, preferred_element_type=jnp.float32)
    activated = (jax.nn.silu(gate_act) * up_act).astype(jnp.bfloat16)
    feed = lax.dot_general(activated, down_weight, (((1,), (1,)), ((), ())), preferred_element_type=jnp.float32)
    live_rows = (lengths > 0)[:, None]
    return jnp.where(live_rows, residual + feed, 0.0).astype(jnp.bfloat16)
```

```python
import jax
import jax.numpy as jnp
from jax import lax
from jax.sharding import PartitionSpec as P

BF16 = jnp.bfloat16
F32 = jnp.float32
EPS = 1e-05


def attend(query, key_cache, value_cache, lengths):
    slot_count = query.shape[0]
    head_dim = key_cache.shape[2]
    head_count = query.shape[1] // head_dim
    queries = query.reshape(slot_count, head_count, head_dim)
    scores = jnp.einsum(
        "shd,std->sht", queries, key_cache, preferred_element_type=jnp.float32
    ) * head_dim ** (-0.5)
    positions = lax.broadcasted_iota(jnp.int32, (1, 1, key_cache.shape[1]), 2)
    in_range = positions < jnp.maximum(lengths, 1)[:, None, None]
    scores = jnp.where(in_range, scores, -jnp.inf)
    highest = jnp.max(scores, axis=2, keepdims=True)
    weights = jnp.exp(scores - highest)
    probs = (weights / jnp.sum(weights, axis=2, keepdims=True)).astype(jnp.bfloat16)
    attended = jnp.einsum("sht,std->shd", probs, value_cache, preferred_element_type=jnp.float32)
    return attended.reshape(slot_count, head_count * head_dim).astype(jnp.bfloat16)


def make_shards(groups, devs):
    chips = devs // 2
    peers = groups * chips
    plane = [[2 * k + c for k in range(chips)] for c in range(2)]
    cube = [[2 * k + c for k in range(peers)] for c in range(2)]
    other = [(i, i ^ 1) for i in range(devs)]

    def shards(
        query,
        key_cache,
        value_cache,
        lengths,
        hidden,
        out_weight,
        ffn_gain,
        gate_weight,
        up_weight,
        down_weight,
    ):
        me = lax.axis_index("dev")
        core = lax.rem(me, 2)
        chip = lax.div(me, 2)
        slots, width = hidden.shape
        cols = width // chips

        def swap(w):
            return lax.ppermute(w, "dev", other)

        out_other = swap(out_weight)
        gate_other = swap(gate_weight)
        up_other = swap(up_weight)
        down_other = swap(down_weight)

        attended = attend(query, key_cache, value_cache, lengths)
        kdim = attended.shape[1]
        pieces = hidden.reshape(slots, chips, cols).transpose(1, 0, 2)
        message = jnp.concatenate(
            [jnp.broadcast_to(attended[None], (chips, slots, kdim)), pieces], axis=2
        )
        got = lax.all_to_all(message, "dev", 0, 0, axis_index_groups=plane)
        got = got.reshape(chips * slots, kdim + cols)
        rows_in, hid = got[:, :kdim], got[:, kdim:]

        own = jnp.dot(rows_in, out_weight, preferred_element_type=F32).astype(BF16)
        oth = jnp.dot(rows_in, out_other, preferred_element_type=F32).astype(BF16)
        first = jnp.where(core == 0, own, oth)
        second = jnp.where(core == 0, oth, own)
        projected = jnp.concatenate([first, second], axis=1)
        residual = hid.astype(F32) + projected.astype(F32)
        gain = lax.dynamic_slice(ffn_gain, (chip * cols,), (cols,))
        sent = (residual * gain).astype(BF16)
        block = jnp.broadcast_to(sent[None], (peers,) + sent.shape)
        blocks = lax.all_to_all(block, ("grp", "dev"), 0, 0, axis_index_groups=cube)
        x = blocks.reshape(groups, chips, chips * slots, cols).transpose(0, 2, 1, 3)
        x = x.reshape(groups * chips * slots, width)

        res = x.astype(F32) / ffn_gain
        scale = lax.rsqrt(jnp.mean(res * res, axis=1, keepdims=True) + EPS)

        def wide(a, b):
            return jnp.concatenate(
                [jnp.dot(x, a, preferred_element_type=F32), jnp.dot(x, b, preferred_element_type=F32)], axis=1
            )

        gate_act = wide(gate_weight, gate_other) * scale
        up_act = wide(up_weight, up_other) * scale
        activated = (jax.nn.silu(gate_act) * up_act).astype(BF16)
        down = jnp.concatenate([down_weight, down_other], axis=1)
        partial = lax.dot_general(
            activated, down, (((1,), (1,)), ((), ())), preferred_element_type=F32
        ).astype(BF16)
        parts = lax.all_to_all(
            partial.reshape(peers, slots, width), ("grp", "dev"), 0, 0, axis_index_groups=cube
        )
        feed = jnp.sum(parts.astype(F32), axis=0)
        mine = lax.dynamic_slice(
            res, ((lax.axis_index("grp") * chips + chip) * slots, 0), (slots, width)
        )
        live_rows = (lengths > 0)[:, None]
        return jnp.where(live_rows, mine + feed, 0.0).astype(BF16)

    return shards


def solution(mesh):
    both = ("grp", "dev")
    in_specs = (
        P(both, None),
        P(both, None, None),
        P(both, None, None),
        P(both),
        P(both, None),
        P(None, "dev"),
        P(),
        P(None, both),
        P(None, both),
        P(None, both),
    )
    body = make_shards(mesh.shape["grp"], mesh.shape["dev"])
    return jax.shard_map(body, mesh=mesh, in_specs=in_specs, out_specs=P(both, None), check_vma=False)
```

```python
import functools

import jax
import jax.numpy as jnp
from jax import lax
from jax.experimental import pallas as pl
from jax.experimental.pallas import tpu as pltpu
from jax.sharding import PartitionSpec as P

BF16 = jnp.bfloat16
F32 = jnp.float32
EPS = 1e-05
NT = (((1,), (1,)), ((), ()))


def attend(query, key_cache, value_cache, lengths):
    slot_count = query.shape[0]
    head_dim = key_cache.shape[2]
    head_count = query.shape[1] // head_dim
    queries = query.reshape(slot_count, head_count, head_dim)
    scores = jnp.einsum(
        "shd,std->sht", queries, key_cache, preferred_element_type=jnp.float32
    ) * head_dim ** (-0.5)
    positions = lax.broadcasted_iota(jnp.int32, (1, 1, key_cache.shape[1]), 2)
    in_range = positions < jnp.maximum(lengths, 1)[:, None, None]
    scores = jnp.where(in_range, scores, -jnp.inf)
    highest = jnp.max(scores, axis=2, keepdims=True)
    weights = jnp.exp(scores - highest)
    probs = (weights / jnp.sum(weights, axis=2, keepdims=True)).astype(jnp.bfloat16)
    attended = jnp.einsum("sht,std->shd", probs, value_cache, preferred_element_type=jnp.float32)
    return attended.reshape(slot_count, head_count * head_dim).astype(jnp.bfloat16)


def project_kernel(steps, cols, x_ref, own_ref, oth_ref, hid_ref, gain_ref, out_ref, acc_own, acc_oth):
    k = pl.program_id(0)

    @pl.when(k == 0)
    def _():
        acc_own[...] = jnp.zeros_like(acc_own)
        acc_oth[...] = jnp.zeros_like(acc_oth)

    x = x_ref[...]
    acc_own[...] += lax.dot_general(x, own_ref[...], NT, preferred_element_type=F32)
    acc_oth[...] += lax.dot_general(x, oth_ref[...], NT, preferred_element_type=F32)

    @pl.when(k == steps - 1)
    def _():
        rows = x_ref.shape[0]
        pad = jnp.zeros((rows, 256 - cols), F32)

        def half(acc, at):
            projected = acc[...].astype(BF16).astype(F32)
            projected = jnp.concatenate([projected, pad], axis=1)
            return hid_ref[:, at : at + 256].astype(F32) + projected

        first, second = half(acc_own, 0), half(acc_oth, 256)
        squares = jnp.sum(first * first, axis=1, keepdims=True) + jnp.sum(
            second * second, axis=1, keepdims=True
        )
        high = squares.astype(BF16).astype(F32)
        low = squares - high
        lane = lax.broadcasted_iota(jnp.int32, (rows, 256), 1)
        sent = first * gain_ref[:, :256]
        sent = jnp.where(lane == cols, high, jnp.where(lane == cols + 1, low, sent))
        block = jnp.concatenate([sent, second * gain_ref[:, 256:]], axis=1).astype(BF16)
        for p in range(out_ref.shape[0]):
            out_ref[p] = block


def project(rows_in, hid, gain, out_own, out_oth, peers):
    rows = rows_in.shape[0]
    cols, depth = out_own.shape
    chunk = 2048
    steps = depth // chunk
    return pl.pallas_call(
        functools.partial(project_kernel, steps, cols),
        grid=(steps,),
        in_specs=[
            pl.BlockSpec((rows, chunk), lambda k: (0, k)),
            pl.BlockSpec((cols, chunk), lambda k: (0, k)),
            pl.BlockSpec((cols, chunk), lambda k: (0, k)),
            pl.BlockSpec((rows, 512), lambda k: (0, 0)),
            pl.BlockSpec((1, 512), lambda k: (0, 0)),
        ],
        out_specs=pl.BlockSpec((peers, rows, 512), lambda k: (0, 0, 0)),
        out_shape=jax.ShapeDtypeStruct((peers, rows, 512), BF16),
        scratch_shapes=[pltpu.VMEM((rows, cols), F32), pltpu.VMEM((rows, cols), F32)],
        compiler_params=pltpu.CompilerParams(vmem_limit_bytes=32 * 2**20),
        cost_estimate=pl.CostEstimate(
            flops=4 * rows * cols * depth, bytes_accessed=4 * cols * depth, transcendentals=0
        ),
    )(rows_in, out_own, out_oth, hid, gain)


def ffn_kernel(
    steps1, steps2, per1, per2, cols, width,
    core_ref, x_ref, go_ref, gx_ref, uo_ref, ux_ref, do_ref, dx_ref,
    out_ref, acc, sq, act, held,
):
    s = pl.program_id(0)
    groups, _, rows, _ = x_ref.shape
    total = groups * rows
    units = go_ref.shape[1]

    @pl.when(s == 0)
    def _():
        acc[...] = jnp.zeros_like(acc)
        sq[...] = jnp.zeros_like(sq)

    @pl.when(s < steps1)
    def _():
        core = core_ref[0]
        sums = acc[...]
        tails = sq[...]
        for b in range(per1):
            x = x_ref[:, b].reshape(total, 512)
            at_own = pl.multiple_of(2 * cols * b + cols * core, 32)
            at_oth = pl.multiple_of(2 * cols * b + cols * (1 - core), 32)
            for at, lo in ((at_own, 0), (at_oth, 256)):
                w = jnp.concatenate(
                    [r[pl.ds(at, cols), :] for r in (go_ref, gx_ref, uo_ref, ux_ref)], axis=1
                )
                sums += jnp.dot(x[:, lo : lo + cols], w, preferred_element_type=F32)
            tails += x[:, 128:256].astype(F32)
        acc[...] = sums
        sq[...] = tails

    @pl.when(s == steps1 - 1)
    def _():
        lane = lax.broadcasted_iota(jnp.int32, (total, 128), 1)
        keep = (lane == cols - 128) | (lane == cols - 127)
        squares = jnp.sum(jnp.where(keep, sq[...], 0.0), axis=1, keepdims=True)
        scale = lax.rsqrt(squares / width + EPS)
        gate = acc[:, : 2 * units] * scale
        up = acc[:, 2 * units :] * scale
        act[...] = (gate / (1.0 + jnp.exp(-gate)) * up).astype(BF16)

    @pl.when(s >= steps1)
    def _():
        span = held.shape[2]
        a = act[...]
        for b in range(per2):
            w = jnp.concatenate(
                [do_ref[b * span : (b + 1) * span, :], dx_ref[b * span : (b + 1) * span, :]], axis=1
            )
            y = lax.dot_general(a, w, NT, preferred_element_type=F32)
            held[(s - steps1) * per2 + b] = y.astype(BF16)

    @pl.when(s == steps1 + steps2 - 1)
    def _():
        spans, _, span = held.shape
        slots = 16 // spans
        r = lax.broadcasted_iota(jnp.int32, (128, 128), 0)
        q = lax.broadcasted_iota(jnp.int32, (128, 128), 1)
        peer, piece, slot = r // 16, (r // slots) % spans, r % slots
        order = jnp.where(q == piece * 16 + peer * slots + slot, 1.0, 0.0).astype(BF16)
        for g in range(total // 16):
            stack = jnp.concatenate([held[b, g * 16 : (g + 1) * 16, :] for b in range(spans)], axis=0)
            moved = jnp.dot(order, stack, preferred_element_type=F32).astype(BF16)
            out_ref[g * 8 : (g + 1) * 8] = moved.reshape(8, 16, span)


def feed_forward(core, blocks, gate, up, down, chips, slots):
    peers, rows, _ = blocks.shape
    groups = peers // chips
    total = groups * rows
    width, units = gate[0].shape
    cols = width // chips // 2
    per1, per2, spans = 4, 2, 16 // slots
    steps1, steps2 = chips // per1, spans // per2
    span = width // spans
    x = blocks.reshape(groups, chips, rows, 512)
    in1 = pl.BlockSpec((per1 * 2 * cols, units), lambda s: (jnp.minimum(s, steps1 - 1), 0))
    in2 = pl.BlockSpec((per2 * span, units), lambda s: (jnp.maximum(s - steps1, 0), 0))
    return pl.pallas_call(
        functools.partial(ffn_kernel, steps1, steps2, per1, per2, cols, width),
        grid=(steps1 + steps2,),
        in_specs=[
            pl.BlockSpec(memory_space=pltpu.SMEM),
            pl.BlockSpec((groups, per1, rows, 512), lambda s: (0, jnp.minimum(s, steps1 - 1), 0, 0)),
            in1, in1, in1, in1, in2, in2,
        ],
        out_specs=pl.BlockSpec((peers, 16, span), lambda s: (0, 0, 0)),
        out_shape=jax.ShapeDtypeStruct((peers, 16, span), BF16),
        scratch_shapes=[
            pltpu.VMEM((total, 4 * units), F32),
            pltpu.VMEM((total, 128), F32),
            pltpu.VMEM((total, 2 * units), BF16),
            pltpu.VMEM((spans, total, span), BF16),
        ],
        compiler_params=pltpu.CompilerParams(vmem_limit_bytes=40 * 2**20),
        cost_estimate=pl.CostEstimate(
            flops=12 * total * units * width, bytes_accessed=14 * width * units, transcendentals=0
        ),
    )(core, x, gate[0], gate[1], up[0], up[1], down[0], down[1])


def final_kernel(lengths_ref, parts_ref, res_ref, out_ref):
    total = res_ref[...]
    for p in range(parts_ref.shape[0]):
        total += parts_ref[p].astype(F32)
    row = lax.broadcasted_iota(jnp.int32, total.shape, 0)
    live = jnp.where(row % 2 == 0, lengths_ref[0], lengths_ref[1]) > 0
    out_ref[...] = jnp.where(live, total, 0.0).astype(BF16)


def finish(lengths, parts, res):
    vmem = pl.BlockSpec(memory_space=pltpu.VMEM)
    return pl.pallas_call(
        final_kernel,
        in_specs=[pl.BlockSpec(memory_space=pltpu.SMEM), vmem, vmem],
        out_specs=vmem,
        out_shape=jax.ShapeDtypeStruct(res.shape, BF16),
        compiler_params=pltpu.CompilerParams(vmem_limit_bytes=16 * 2**20),
    )(lengths, parts, res)


def make_shards(groups, devs):
    chips = devs // 2
    peers = groups * chips
    plane = [[2 * k + c for k in range(chips)] for c in range(2)]
    cube = [[2 * k + c for k in range(peers)] for c in range(2)]
    other = [(i, i ^ 1) for i in range(devs)]

    def shards(
        query,
        key_cache,
        value_cache,
        lengths,
        hidden,
        out_weight,
        ffn_gain,
        gate_weight,
        up_weight,
        down_weight,
    ):
        me = lax.axis_index("dev")
        core = lax.rem(me, 2)
        chip = lax.div(me, 2)
        slots, width = hidden.shape
        cols = width // devs

        def swap(w):
            return lax.ppermute(w, "dev", other)

        out_own = out_weight.T
        out_oth = swap(out_own)
        gate_oth = swap(gate_weight)
        up_oth = swap(up_weight)
        down_oth = swap(down_weight)

        def halves(v):
            v = v.reshape(v.shape[0], chips, 2, cols)
            v = jnp.where(core == 0, v, v[:, :, ::-1])
            return jnp.pad(v, ((0, 0), (0, 0), (0, 0), (0, 256 - cols))).reshape(v.shape[0], chips, 512)

        attended = attend(query, key_cache, value_cache, lengths)
        kdim = attended.shape[1]
        message = jnp.concatenate(
            [
                jnp.broadcast_to(attended[None], (chips, slots, kdim)),
                halves(hidden).transpose(1, 0, 2),
            ],
            axis=2,
        )
        got = lax.all_to_all(message, "dev", 0, 0, axis_index_groups=plane)
        got = got.reshape(chips * slots, kdim + 512)
        gains = halves(ffn_gain.reshape(1, width))
        gain = lax.dynamic_slice(gains, (0, chip, 0), (1, 1, 512)).reshape(1, 512)
        block = project(got, got[:, kdim:], gain, out_own, out_oth, peers)
        blocks = lax.all_to_all(block, ("grp", "dev"), 0, 0, axis_index_groups=cube)

        partial = feed_forward(
            core.reshape(1),
            blocks,
            (gate_weight, gate_oth),
            (up_weight, up_oth),
            (down_weight, down_oth),
            chips,
            slots,
        )
        parts = lax.all_to_all(partial, ("grp", "dev"), 0, 0, axis_index_groups=cube)

        mine = lax.dynamic_slice(
            blocks, (lax.axis_index("grp") * chips, chip * slots, 0), (chips, slots, 512)
        )
        mine = mine.reshape(chips, slots, 2, 256)[:, :, :, :cols].astype(F32)
        mine = jnp.where(core == 0, mine, mine[:, :, ::-1])
        mine = mine.transpose(1, 0, 2, 3).reshape(slots, width) / ffn_gain
        spans = 16 // slots
        mine = mine.reshape(slots, spans, width // spans).transpose(1, 0, 2).reshape(16, width // spans)
        out = finish(lengths, parts, mine)
        return out.reshape(spans, slots, width // spans).transpose(1, 0, 2).reshape(slots, width)

    return shards


def solution(mesh):
    both = ("grp", "dev")
    in_specs = (
        P(both, None),
        P(both, None, None),
        P(both, None, None),
        P(both),
        P(both, None),
        P(None, "dev"),
        P(),
        P(None, both),
        P(None, both),
        P(None, both),
    )
    body = make_shards(mesh.shape["grp"], mesh.shape["dev"])
    return jax.shard_map(body, mesh=mesh, in_specs=in_specs, out_specs=P(both, None), check_vma=False)
```

```python
import functools

import jax
import jax.numpy as jnp
from jax import lax
from jax.experimental import pallas as pl
from jax.experimental.pallas import tpu as pltpu
from jax.sharding import PartitionSpec as P

BF16 = jnp.bfloat16
F32 = jnp.float32
EPS = 1e-05
VMEM = 40 * 2**20
NT = (((1,), (1,)), ((), ()))


def attend_kernel(lengths_ref, q_ref, k_hbm, v_hbm, hid_ref, out_ref, keys, values, sems):
    slots, span, dim = keys.shape
    heads = q_ref.shape[1] // dim
    chips = out_ref.shape[0]
    copies = []
    for i, (src, dst) in enumerate(((k_hbm, keys), (v_hbm, values))):
        for s in range(slots):
            copy = pltpu.make_async_copy(src.at[s], dst.at[s], sems.at[i, s])
            copy.start()
            copies.append(copy)
    q = q_ref[...].astype(F32)
    q = jnp.concatenate(
        [q[s : s + 1, h * dim : (h + 1) * dim] for s in range(slots) for h in range(heads)], axis=0
    ).astype(BF16)
    hid = hid_ref[...].astype(F32)
    row = lax.broadcasted_iota(jnp.int32, (16, 128), 0)
    tiles = [
        jnp.where(row % slots == 0, hid[0:1, t * 128 : (t + 1) * 128], hid[1:2, t * 128 : (t + 1) * 128])
        for t in range(hid.shape[1] // 128)
    ]
    extra = []
    for p in range(chips):
        first = (p * hid.shape[1] // chips) // 128
        held = jnp.zeros((16, 128), F32)
        for i in range(4):
            held = jnp.where(row // slots == i, tiles[first + i], held)
        extra.append(held.astype(BF16))
    parts, totals = [], []
    position = lax.broadcasted_iota(jnp.int32, (heads, span), 1)
    for s in range(slots):
        copies[s].wait()
        scores = lax.dot_general(
            q[s * heads : (s + 1) * heads, :], keys[s], NT, preferred_element_type=F32
        ) * dim ** (-0.5)
        scores = jnp.where(position < jnp.maximum(lengths_ref[s], 1), scores, -jnp.inf)
        weights = jnp.exp(scores - jnp.max(scores, axis=1, keepdims=True))
        totals.append(jnp.sum(weights, axis=1, keepdims=True))
        parts.append(weights.astype(BF16))
    for s in range(slots):
        copies[slots + s].wait()
        attended = jnp.dot(parts[s], values[s], preferred_element_type=F32)
        parts[s] = (attended / totals[s]).astype(BF16)
    both = jnp.concatenate(parts, axis=0)
    pieces = 16 // slots
    per = heads // pieces
    r = lax.broadcasted_iota(jnp.int32, (16, slots * heads), 0)
    c = lax.broadcasted_iota(jnp.int32, (16, slots * heads), 1)
    rows = []
    for j in range(per):
        take = jnp.where(c == (r % slots) * heads + (r // slots) * per + j, 1.0, 0.0).astype(BF16)
        rows.append(jnp.dot(take, both, preferred_element_type=F32).astype(BF16))
    rows = jnp.concatenate(rows, axis=1)
    for p in range(chips):
        out_ref[p] = jnp.concatenate([rows, extra[p]], axis=1)


def attend(lengths, query, key_cache, value_cache, hidden, chips):
    slots, span, dim = key_cache.shape
    hbm = pl.BlockSpec(memory_space=pl.ANY)
    vmem = pl.BlockSpec(memory_space=pltpu.VMEM)
    lanes = query.shape[1] * slots // 16 + 128
    return pl.pallas_call(
        attend_kernel,
        in_specs=[pl.BlockSpec(memory_space=pltpu.SMEM), vmem, hbm, hbm, vmem],
        out_specs=vmem,
        out_shape=pltpu.HBM((chips, 16, lanes), BF16),
        scratch_shapes=[
            pltpu.VMEM(key_cache.shape, BF16),
            pltpu.VMEM(value_cache.shape, BF16),
            pltpu.SemaphoreType.DMA((2, slots)),
        ],
        compiler_params=pltpu.CompilerParams(vmem_limit_bytes=58 * 2**20),
    )(lengths, query, key_cache, value_cache, hidden)


def project_kernel(
    cols, where_ref, x_hbm, own_hbm, oth_hbm, gain_ref, out_hbm, x_buf, own, oth, block, sems, out_sem
):
    chips, deep, lanes = x_buf.shape
    depth = own.shape[1]
    slots = 2
    pieces = deep // slots
    rows = chips * slots
    cut = 128
    first = pltpu.make_async_copy(x_hbm, x_buf, sems.at[0])
    copies = [
        pltpu.make_async_copy(src.at[span], dst.at[span], sems.at[1 + 2 * i + j])
        for i, (src, dst) in enumerate(((own_hbm, own), (oth_hbm, oth)))
        for j, span in enumerate((pl.ds(0, cut), pl.ds(cut, cols - cut)))
    ]
    first.start()
    copies[0].start()
    copies[1].start()
    r = lax.broadcasted_iota(jnp.int32, (chips * deep, chips * deep), 0)
    c = lax.broadcasted_iota(jnp.int32, (chips * deep, chips * deep), 1)
    order = c == (r % rows) // slots * deep + r // rows * slots + r % slots
    order = jnp.where(order, 1.0, 0.0).astype(BF16)
    first.wait()
    x = jnp.dot(order, x_buf[...].reshape(chips * deep, lanes), preferred_element_type=F32)
    wide = depth // pieces
    chip = where_ref[1]
    lane = lax.broadcasted_iota(jnp.int32, (rows, 128), 1)

    def ahead(tiles, shift):
        moved = [pltpu.roll(t, 128 - shift, 1) for t in tiles]
        return [jnp.where(lane < 128 - shift, a, b) for a, b in zip(moved, moved[1:] + moved[-1:])]

    hids = [x[i * rows : (i + 1) * rows, wide : wide + 128] for i in range(4)]
    hids = [jnp.where(chip % 2 == 0, a, b) for a, b in zip(hids, ahead(hids, 64))]
    hid_a = jnp.concatenate(hids[:2], axis=1)
    hid_b = jnp.concatenate(ahead(hids[1:], cols - 128)[:2], axis=1)
    x = jnp.concatenate([x[i * rows : (i + 1) * rows, :wide] for i in range(pieces)], axis=1).astype(BF16)
    copies[0].wait()
    copies[2].start()
    copies[1].wait()
    copies[3].start()
    sums = [lax.dot_general(x, own[...], NT, preferred_element_type=F32)]
    copies[2].wait()
    copies[3].wait()
    sums.append(lax.dot_general(x, oth[...], NT, preferred_element_type=F32))
    pad = jnp.zeros((rows, 256 - cols), F32)
    swapped = where_ref[0] == 1
    hids = (jnp.where(swapped, hid_b, hid_a), jnp.where(swapped, hid_a, hid_b))
    gains = gain_ref[pl.ds(chip, 1), :]
    sent = []
    for i in range(2):
        projected = jnp.concatenate([sums[i].astype(BF16).astype(F32), pad], axis=1)
        sent.append((hids[i] + projected) * gains[:, 256 * i : 256 * i + 256])
    own_tail, oth_tail = sent[0][:, 128:], sent[1][:, 128:]
    third = jnp.where(lane < cols - 128, own_tail, pltpu.roll(oth_tail, cols - 128, 1))
    rest = pltpu.roll(oth_tail, 128 - (256 - cols), 1)
    turned = pltpu.roll(rest, 64, 1)
    half = rows // 2
    low = lax.broadcasted_iota(jnp.int32, (half, 128), 1) < 64
    even = jnp.where(low, rest[:half], turned[half:])
    odd = jnp.where(low, rest[half:], turned[:half])
    last = jnp.where(chip % 2 == 0, even, odd)
    packed = jnp.concatenate([sent[0][:, :128], sent[1][:, :128], third, last], axis=0).astype(BF16)
    copies = block.shape[0]
    for p in range(copies):
        block[p] = packed
    outs = []
    for p in range(out_hbm.shape[0] // copies):
        out = pltpu.make_async_copy(block, out_hbm.at[pl.ds(p * copies, copies)], out_sem.at[p])
        out.start()
        outs.append(out)
    for out in outs:
        out.wait()


def in_hbm(v):
    return pltpu.with_memory_space_constraint(v, pltpu.HBM)


def project(where, messages, gains, out_own, out_oth, peers):
    cols, depth = out_own.shape
    rows = messages.shape[0] * 2
    packed = rows * 2 * cols // 128
    hbm = pl.BlockSpec(memory_space=pl.ANY)
    vmem = pl.BlockSpec(memory_space=pltpu.VMEM)
    return pl.pallas_call(
        functools.partial(project_kernel, cols),
        in_specs=[pl.BlockSpec(memory_space=pltpu.SMEM), hbm, hbm, hbm, vmem],
        out_specs=hbm,
        out_shape=pltpu.HBM((peers, packed, 128), BF16),
        scratch_shapes=[
            pltpu.VMEM(messages.shape, BF16),
            pltpu.VMEM((cols, depth), BF16),
            pltpu.VMEM((cols, depth), BF16),
            pltpu.VMEM((8, packed, 128), BF16),
            pltpu.SemaphoreType.DMA((5,)),
            pltpu.SemaphoreType.DMA((peers // 8,)),
        ],
        compiler_params=pltpu.CompilerParams(vmem_limit_bytes=VMEM),
        cost_estimate=pl.CostEstimate(
            flops=4 * rows * cols * depth, bytes_accessed=4 * cols * depth, transcendentals=0
        ),
    )(where, messages, in_hbm(out_own), in_hbm(out_oth), gains)


def ffn_kernel(
    chips, cols, width,
    where_ref, x_hbm, go_hbm, gx_hbm, uo_hbm, ux_hbm, do_hbm, dx_hbm, ig_ref, out_hbm,
    x_buf, wide, down, held, out_buf, x_sem, wide_sem, down_sem, out_sem,
):
    groups, _, packed, _ = x_buf.shape
    rows = packed * 128 // (2 * cols)
    total = groups * rows
    units = wide.shape[2]
    quarter = 4
    parts = chips // quarter
    deep = quarter * 2 * cols
    core = where_ref[0]

    spans, _, span = held.shape
    stages = []
    for q in range(parts):
        chip_span, deep_span = pl.ds(q * quarter, quarter), pl.ds(q * deep, deep)
        stages.append(
            [pltpu.make_async_copy(x_hbm.at[:, chip_span], x_buf.at[:, chip_span], x_sem.at[q])]
            + [
                pltpu.make_async_copy(src.at[deep_span], wide.at[i, deep_span], wide_sem.at[i, q])
                for i, src in enumerate((go_hbm, gx_hbm, uo_hbm, ux_hbm))
            ]
        )
    for q in range(parts):
        some = pl.ds(q * deep, deep)
        stages.append(
            [
                pltpu.make_async_copy(src.at[some], down.at[i, some], down_sem.at[i, q])
                for i, src in enumerate((do_hbm, dx_hbm))
            ]
        )

    def begin(k):
        for copy in stages[k]:
            copy.start()

    def arrive(k):
        for copy in stages[k]:
            copy.wait()
        if k + parts < len(stages):
            begin(k + parts)

    for k in range(parts):
        begin(k)

    sums = jnp.zeros((total, 4 * units), F32)
    squares = jnp.zeros((total, 128), F32)
    half = rows // 2
    low = lax.broadcasted_iota(jnp.int32, (groups, half, 128), 2) < 64
    for q in range(parts):
        arrive(q)

        def weights(at, size):
            return jnp.concatenate([wide[i, pl.ds(at, size), :] for i in range(4)], axis=1)

        tiles, stacks = [], []
        for b in range(q * quarter, (q + 1) * quarter):
            own = pl.multiple_of(2 * cols * b + cols * core, 32)
            oth = pl.multiple_of(2 * cols * b + cols * (1 - core), 32)
            tiles += [x_buf[:, b, i * rows : (i + 1) * rows, :].reshape(total, 128) for i in range(3)]
            stacks += [
                weights(own, 128),
                weights(oth, 128),
                weights(pl.multiple_of(own + 128, 32), cols - 128),
                weights(pl.multiple_of(oth + 128, 32), 256 - cols),
            ]
        for b in range(q * quarter, (q + 1) * quarter, 2):
            first, second = (x_buf[:, b + i, 3 * rows :, :].astype(F32) for i in range(2))
            top = jnp.where(low, first, second)
            bottom = jnp.where(low, second, first)
            bottom = pltpu.roll(bottom.reshape(groups * half, 128), 64, 1).reshape(groups, half, 128)
            tiles.append(jnp.concatenate([top, bottom], axis=1).reshape(total, 128).astype(BF16))
            for i in range(2):
                oth = pl.multiple_of(2 * cols * (b + i) + cols * (1 - core) + (384 - cols), 32)
                stacks.append(weights(oth, 2 * cols - 384))
        x = jnp.concatenate(tiles, axis=1)
        sums += jnp.dot(x, jnp.concatenate(stacks, axis=0), preferred_element_type=F32)
        for i, tile in enumerate(tiles):
            res = tile.astype(F32) * ig_ref[q * len(tiles) + i : q * len(tiles) + i + 1, :]
            squares += res * res

    scale = lax.rsqrt(jnp.sum(squares, axis=1, keepdims=True) / width + EPS)
    gate = sums[:, : 2 * units] * scale
    up = sums[:, 2 * units :] * scale
    act = (gate / (1.0 + jnp.exp(-gate)) * up).astype(BF16)

    for b in range(spans):
        if b % (spans // parts) == 0:
            arrive(parts + b // (spans // parts))
        some = slice(b * span, (b + 1) * span)
        w = jnp.concatenate([down[0, some, :], down[1, some, :]], axis=1)
        held[b] = lax.dot_general(act, w, NT, preferred_element_type=F32).astype(BF16)

    r = lax.broadcasted_iota(jnp.int32, (128, 128), 0)
    c = lax.broadcasted_iota(jnp.int32, (128, 128), 1)
    peer, piece, slot = r // 16, (r // 2) % spans, r % 2
    order = jnp.where(c == piece * 16 + peer * 2 + slot, 1.0, 0.0).astype(BF16)
    outs = []
    for g in range(total // 16):
        stack = jnp.concatenate([held[b, g * 16 : (g + 1) * 16, :] for b in range(spans)], axis=0)
        moved = jnp.dot(order, stack, preferred_element_type=F32).astype(BF16)
        some = pl.ds(g * 8, 8)
        out_buf[g * 8 : (g + 1) * 8] = moved.reshape(8, 16, span)
        outs.append(pltpu.make_async_copy(out_buf.at[some], out_hbm.at[some], out_sem.at[g]))
        outs[-1].start()
    for out in outs:
        out.wait()


def feed_forward(where, blocks, gate, up, down, inverse_gain, chips):
    peers, packed, _ = blocks.shape
    groups = peers // chips
    width, units = gate[0].shape
    cols = width // chips // 2
    rows = packed * 128 // (2 * cols)
    total = groups * rows
    spans, parts = 8, 4
    span = width // spans
    hbm = pl.BlockSpec(memory_space=pl.ANY)
    return pl.pallas_call(
        functools.partial(ffn_kernel, chips, cols, width),
        in_specs=[pl.BlockSpec(memory_space=pltpu.SMEM)]
        + [hbm] * 7
        + [pl.BlockSpec(memory_space=pltpu.VMEM)],
        out_specs=hbm,
        out_shape=pltpu.HBM((peers, 16, span), BF16),
        scratch_shapes=[
            pltpu.VMEM((groups, chips, packed, 128), BF16),
            pltpu.VMEM((4, width, units), BF16),
            pltpu.VMEM((2, width, units), BF16),
            pltpu.VMEM((spans, total, span), BF16),
            pltpu.VMEM((peers, 16, span), BF16),
            pltpu.SemaphoreType.DMA((parts,)),
            pltpu.SemaphoreType.DMA((4, parts)),
            pltpu.SemaphoreType.DMA((2, parts)),
            pltpu.SemaphoreType.DMA((total // 16,)),
        ],
        compiler_params=pltpu.CompilerParams(vmem_limit_bytes=VMEM),
        cost_estimate=pl.CostEstimate(
            flops=12 * total * units * width, bytes_accessed=14 * width * units, transcendentals=0
        ),
    )(
        where,
        blocks.reshape(groups, chips, packed, 128),
        *[in_hbm(v) for v in (*gate, *up, *down)],
        inverse_gain,
    )


def final_kernel(lengths_ref, parts_hbm, res_ref, out_ref, parts, sems):
    quarter = parts.shape[0] // 4
    copies = []
    for q in range(4):
        some = pl.ds(q * quarter, quarter)
        copies.append(pltpu.make_async_copy(parts_hbm.at[some], parts.at[some], sems.at[q]))
        copies[q].start()
    total = res_ref[...]
    for q in range(4):
        copies[q].wait()
        for p in range(q * quarter, (q + 1) * quarter):
            total += parts[p].astype(F32)
    row = lax.broadcasted_iota(jnp.int32, total.shape, 0)
    live = jnp.where(row % 2 == 0, lengths_ref[0], lengths_ref[1]) > 0
    out_ref[...] = jnp.where(live, total, 0.0).astype(BF16)


def finish(lengths, parts, res):
    vmem = pl.BlockSpec(memory_space=pltpu.VMEM)
    return pl.pallas_call(
        final_kernel,
        in_specs=[pl.BlockSpec(memory_space=pltpu.SMEM), pl.BlockSpec(memory_space=pl.ANY), vmem],
        out_specs=vmem,
        out_shape=jax.ShapeDtypeStruct(res.shape, BF16),
        scratch_shapes=[pltpu.VMEM(parts.shape, BF16), pltpu.SemaphoreType.DMA((4,))],
        compiler_params=pltpu.CompilerParams(vmem_limit_bytes=16 * 2**20),
    )(lengths, parts, res)


def make_shards(groups, devs):
    chips = devs // 2
    peers = groups * chips
    plane = [[2 * k + c for k in range(chips)] for c in range(2)]
    cube = [[2 * k + c for k in range(peers)] for c in range(2)]
    other = [(i, i ^ 1) for i in range(devs)]

    def shards(
        query,
        key_cache,
        value_cache,
        lengths,
        hidden,
        out_weight,
        ffn_gain,
        gate_weight,
        up_weight,
        down_weight,
    ):
        me = lax.axis_index("dev")
        core = lax.rem(me, 2)
        chip = lax.div(me, 2)
        slots, width = hidden.shape
        cols = width // devs

        def swap(w):
            return lax.ppermute(w, "dev", other)

        out_own = out_weight.T
        out_oth = swap(out_own)
        gate_oth = swap(gate_weight)
        up_oth = swap(up_weight)
        down_oth = swap(down_weight)

        where = jnp.stack([core, chip]).astype(jnp.int32)

        def halves(v):
            v = v.reshape(v.shape[0], chips, 2, cols)
            return jnp.pad(v, ((0, 0), (0, 0), (0, 0), (0, 256 - cols)))

        message = attend(lengths, query, key_cache, value_cache, hidden, chips)
        got = lax.all_to_all(message, "dev", 0, 0, axis_index_groups=plane)
        gain = halves(ffn_gain.reshape(1, width))[0]
        gain = jnp.where(core == 0, gain, gain[:, ::-1])
        block = project(where, got, gain.reshape(chips, 512), out_own, out_oth, peers)
        blocks = lax.all_to_all(block, ("grp", "dev"), 0, 0, axis_index_groups=cube)

        inv = 1.0 / gain
        inv = jnp.concatenate(
            [
                jnp.stack(
                    [
                        inv[:, 0, :128],
                        inv[:, 1, :128],
                        jnp.concatenate([inv[:, 0, 128:cols], inv[:, 1, 128 : 384 - cols]], axis=1),
                    ],
                    axis=1,
                ).reshape(chips // 4, 12, 128),
                inv[:, 1, 384 - cols : cols].reshape(chips // 4, 2, 128),
            ],
            axis=1,
        ).reshape(width // 128, 128)
        partial = feed_forward(
            where,
            blocks,
            (gate_weight, gate_oth),
            (up_weight, up_oth),
            (down_weight, down_oth),
            inv,
            chips,
        )
        parts = lax.all_to_all(partial, ("grp", "dev"), 0, 0, axis_index_groups=cube)

        rows = chips * slots
        mine = lax.dynamic_slice(
            blocks, (lax.axis_index("grp") * chips, 0, 0), (chips,) + blocks.shape[1:]
        )
        full = lax.dynamic_slice(
            mine[:, : 3 * rows].reshape(chips, 3, rows, 128), (0, 0, chip * slots, 0), (chips, 3, slots, 128)
        )
        last = mine[:, 3 * rows :].reshape(chips // 2, 2, rows // 2, 2, 64)
        last = jnp.stack([last[:, 0], last[:, 1, :, ::-1]], axis=1)
        last = last.transpose(0, 1, 3, 2, 4).reshape(chips, rows, 64)
        last = lax.dynamic_slice(last, (0, chip * slots, 0), (chips, slots, 64))
        own = jnp.concatenate([full[:, 0], full[:, 2, :, : cols - 128]], axis=2)
        oth = jnp.concatenate([full[:, 1], full[:, 2, :, cols - 128 :], last], axis=2)
        mine = jnp.stack([jnp.where(core == 0, own, oth), jnp.where(core == 0, oth, own)], axis=2)
        mine = mine.astype(F32).transpose(1, 0, 2, 3).reshape(slots, width) / ffn_gain
        spans = 16 // slots
        mine = mine.reshape(slots, spans, width // spans).transpose(1, 0, 2).reshape(16, width // spans)
        out = finish(lengths, parts, mine)
        return out.reshape(spans, slots, width // spans).transpose(1, 0, 2).reshape(slots, width)

    return shards


def solution(mesh):
    both = ("grp", "dev")
    in_specs = (
        P(both, None),
        P(both, None, None),
        P(both, None, None),
        P(both),
        P(both, None),
        P(None, "dev"),
        P(),
        P(None, both),
        P(None, both),
        P(None, both),
    )
    body = make_shards(mesh.shape["grp"], mesh.shape["dev"])
    return jax.shard_map(body, mesh=mesh, in_specs=in_specs, out_specs=P(both, None), check_vma=False)
```

```python
import functools

import jax
import jax.numpy as jnp
from jax import lax
from jax.experimental import pallas as pl
from jax.experimental.pallas import tpu as pltpu
from jax.sharding import PartitionSpec as P

BF16 = jnp.bfloat16
F32 = jnp.float32
EPS = 1e-05
VMEM = 40 * 2**20
NT = (((1,), (1,)), ((), ()))


def attend_kernel(lengths_ref, q_hbm, k_hbm, v_hbm, hid_hbm, out_ref, q_ref, hid_ref, keys, values, small_sems, sems):
    slots, span, dim = keys.shape
    heads = q_ref.shape[1] // dim
    chips = out_ref.shape[0]
    small = [
        pltpu.make_async_copy(src, dst, small_sems.at[i])
        for i, (src, dst) in enumerate(((q_hbm, q_ref), (hid_hbm, hid_ref)))
    ]
    for copy in small:
        copy.start()
    copies = []
    for i, (src, dst) in enumerate(((k_hbm, keys), (v_hbm, values))):
        for s in range(slots):
            copy = pltpu.make_async_copy(src.at[s], dst.at[s], sems.at[i, s])
            copy.start()
            copies.append(copy)
    small[0].wait()
    q = q_ref[...].astype(F32)
    q = jnp.concatenate(
        [q[s : s + 1, h * dim : (h + 1) * dim] for s in range(slots) for h in range(heads)], axis=0
    ).astype(BF16)
    small[1].wait()
    hid = hid_ref[...].astype(F32)
    row = lax.broadcasted_iota(jnp.int32, (16, 128), 0)
    tiles = [
        jnp.where(row % slots == 0, hid[0:1, t * 128 : (t + 1) * 128], hid[1:2, t * 128 : (t + 1) * 128])
        for t in range(hid.shape[1] // 128)
    ]
    extra = []
    for p in range(chips):
        first = (p * hid.shape[1] // chips) // 128
        held = jnp.zeros((16, 128), F32)
        for i in range(4):
            held = jnp.where(row // slots == i, tiles[first + i], held)
        extra.append(held.astype(BF16))
    parts = []
    position = lax.broadcasted_iota(jnp.int32, (heads, span), 1)
    for s in range(slots):
        copies[s].wait()
        scores = lax.dot_general(
            q[s * heads : (s + 1) * heads, :], keys[s], NT, preferred_element_type=F32
        ) * dim ** (-0.5)
        scores = jnp.where(position < jnp.maximum(lengths_ref[s], 1), scores, -jnp.inf)
        weights = jnp.exp(scores - jnp.max(scores, axis=1, keepdims=True))
        parts.append((weights * (1.0 / jnp.sum(weights, axis=1, keepdims=True))).astype(BF16))
    for s in range(slots):
        copies[slots + s].wait()
        parts[s] = jnp.dot(parts[s], values[s], preferred_element_type=F32).astype(BF16)
    both = jnp.concatenate(parts, axis=0)
    pieces = 16 // slots
    per = heads // pieces
    r = lax.broadcasted_iota(jnp.int32, (16, slots * heads), 0)
    c = lax.broadcasted_iota(jnp.int32, (16, slots * heads), 1)
    rows = []
    for j in range(per):
        take = jnp.where(c == (r % slots) * heads + (r // slots) * per + j, 1.0, 0.0).astype(BF16)
        rows.append(jnp.dot(take, both, preferred_element_type=F32).astype(BF16))
    rows = jnp.concatenate(rows, axis=1)
    for p in range(chips):
        out_ref[p] = jnp.concatenate([rows, extra[p]], axis=1)


def attend(lengths, query, key_cache, value_cache, hidden, chips):
    slots, span, dim = key_cache.shape
    hbm = pl.BlockSpec(memory_space=pl.ANY)
    vmem = pl.BlockSpec(memory_space=pltpu.VMEM)
    lanes = query.shape[1] * slots // 16 + 128
    return pl.pallas_call(
        attend_kernel,
        in_specs=[pl.BlockSpec(memory_space=pltpu.SMEM), hbm, hbm, hbm, hbm],
        out_specs=vmem,
        out_shape=pltpu.HBM((chips, 16, lanes), BF16),
        scratch_shapes=[
            pltpu.VMEM(query.shape, BF16),
            pltpu.VMEM(hidden.shape, BF16),
            pltpu.VMEM(key_cache.shape, BF16),
            pltpu.VMEM(value_cache.shape, BF16),
            pltpu.SemaphoreType.DMA((2,)),
            pltpu.SemaphoreType.DMA((2, slots)),
        ],
        compiler_params=pltpu.CompilerParams(vmem_limit_bytes=12 * 2**20),
    )(in_hbm(lengths), *[in_hbm(v) for v in (query, key_cache, value_cache, hidden)])


def project_kernel(
    steps, cols, x_ref, own_ref, oth_ref, gain_ref, out_hbm, x_rows, hid_rows, acc_own, acc_oth, block, out_sem
):
    step = pl.program_id(0)
    chips, deep, lanes = x_ref.shape
    chunk = own_ref.shape[1]
    slots = 2
    pieces = deep // slots
    rows = chips * slots
    wide = x_rows.shape[1] // pieces

    @pl.when(step == 0)
    def _():
        r = lax.broadcasted_iota(jnp.int32, (chips * deep, chips * deep), 0)
        c = lax.broadcasted_iota(jnp.int32, (chips * deep, chips * deep), 1)
        order = c == (r % rows) // slots * deep + r // rows * slots + r % slots
        order = jnp.where(order, 1.0, 0.0).astype(BF16)
        x = jnp.dot(order, x_ref[...].reshape(chips * deep, lanes), preferred_element_type=F32)
        for i in range(pieces):
            x_rows[:, i * wide : (i + 1) * wide] = x[i * rows : (i + 1) * rows, :wide].astype(BF16)
        for i in range(4):
            hid_rows[i] = x[i * rows : (i + 1) * rows, wide:]

    x = x_rows[:, pl.ds(pl.multiple_of(step * chunk, chunk), chunk)]
    for acc, w in ((acc_own, own_ref), (acc_oth, oth_ref)):
        part = lax.dot_general(x, w[...], NT, preferred_element_type=F32)

        @pl.when(step == 0)
        def _():
            acc[...] = part

        @pl.when(step > 0)
        def _():
            acc[...] += part

    @pl.when(step == steps - 1)
    def _():
        me = lax.axis_index("dev")
        core, chip = me % 2, me // 2
        lane = lax.broadcasted_iota(jnp.int32, (rows, 128), 1)

        def ahead(tiles, shift):
            moved = [pltpu.roll(t, 128 - shift, 1) for t in tiles]
            return [jnp.where(lane < 128 - shift, a, b) for a, b in zip(moved, moved[1:] + moved[-1:])]

        def halves(tiles):
            tiles = [jnp.where(chip % 2 == 0, a, b) for a, b in zip(tiles, ahead(tiles, 64))]
            first = jnp.concatenate(tiles[:2], axis=1)
            second = jnp.concatenate(ahead(tiles[1:], cols - 128)[:2], axis=1)
            return jnp.where(core == 0, first, second), jnp.where(core == 0, second, first)

        hids = halves([hid_rows[i] for i in range(4)])
        start = 7 * (chip // 2) + 3 * (chip % 2)
        gains = halves([jnp.broadcast_to(gain_ref[pl.ds(start + i, 1), :], (rows, 128)) for i in range(4)])
        pad = jnp.zeros((rows, 256 - cols), F32)
        sent = []
        for acc, hid, gain in zip((acc_own, acc_oth), hids, gains):
            projected = jnp.concatenate([acc[...].astype(BF16).astype(F32), pad], axis=1)
            sent.append((hid + projected) * gain)
        own_tail, oth_tail = sent[0][:, 128:], sent[1][:, 128:]
        third = jnp.where(lane < cols - 128, own_tail, pltpu.roll(oth_tail, cols - 128, 1))
        rest = pltpu.roll(oth_tail, 128 - (256 - cols), 1)
        turned = pltpu.roll(rest, 64, 1)
        half = rows // 2
        low = lax.broadcasted_iota(jnp.int32, (half, 128), 1) < 64
        even = jnp.where(low, rest[:half], turned[half:])
        odd = jnp.where(low, rest[half:], turned[:half])
        last = jnp.where(chip % 2 == 0, even, odd)
        packed = jnp.concatenate([sent[0][:, :128], sent[1][:, :128], third, last], axis=0).astype(BF16)
        copies = block.shape[0]
        for p in range(copies):
            block[p] = packed
        outs = []
        for p in range(out_hbm.shape[0] // copies):
            out = pltpu.make_async_copy(block, out_hbm.at[pl.ds(p * copies, copies)], out_sem.at[p])
            out.start()
            outs.append(out)
        for out in outs:
            out.wait()


def in_hbm(v):
    return pltpu.with_memory_space_constraint(v, pltpu.HBM)


def project(messages, gain, out_own, out_oth, peers):
    cols, depth = out_own.shape
    rows = messages.shape[0] * 2
    packed = rows * 2 * cols // 128
    steps = 1
    chunk = depth // steps
    return pl.pallas_call(
        functools.partial(project_kernel, steps, cols),
        grid=(steps,),
        in_specs=[
            pl.BlockSpec(messages.shape, lambda k: (0, 0, 0)),
            pl.BlockSpec((cols, chunk), lambda k: (0, k)),
            pl.BlockSpec((cols, chunk), lambda k: (0, k)),
            pl.BlockSpec(gain.shape, lambda k: (0, 0)),
        ],
        out_specs=pl.BlockSpec(memory_space=pl.ANY),
        out_shape=pltpu.HBM((peers, packed, 128), BF16),
        scratch_shapes=[
            pltpu.VMEM((rows, depth), BF16),
            pltpu.VMEM((4, rows, 128), F32),
            pltpu.VMEM((rows, cols), F32),
            pltpu.VMEM((rows, cols), F32),
            pltpu.VMEM((8, packed, 128), BF16),
            pltpu.SemaphoreType.DMA((peers // 8,)),
        ],
        compiler_params=pltpu.CompilerParams(vmem_limit_bytes=24 * 2**20),
        cost_estimate=pl.CostEstimate(
            flops=4 * rows * cols * depth, bytes_accessed=4 * cols * depth, transcendentals=0
        ),
    )(messages, out_own, out_oth, in_hbm(gain))


def ffn_kernel(
    chips, cols, width,
    x_hbm, go_hbm, gx_hbm, uo_hbm, ux_hbm, do_hbm, dx_hbm, ig_ref, out_hbm,
    x_buf, wide, down, held, out_buf, x_sem, wide_sem, down_sem, out_sem,
):
    groups, _, packed, _ = x_buf.shape
    rows = packed * 128 // (2 * cols)
    total = groups * rows
    units = wide.shape[2]
    quarter = 4
    parts = chips // quarter
    deep = quarter * 2 * cols
    core = lax.axis_index("dev") % 2

    spans, _, span = held.shape
    stages = []
    for q in range(parts):
        chip_span, deep_span = pl.ds(q * quarter, quarter), pl.ds(q * deep, deep)
        stages.append(
            [pltpu.make_async_copy(x_hbm.at[:, chip_span], x_buf.at[:, chip_span], x_sem.at[q])]
            + [
                pltpu.make_async_copy(src.at[deep_span], wide.at[i, deep_span], wide_sem.at[i, q])
                for i, src in enumerate((go_hbm, gx_hbm, uo_hbm, ux_hbm))
            ]
        )
    for q in range(parts):
        some = pl.ds(q * deep, deep)
        stages.append(
            [
                pltpu.make_async_copy(src.at[some], down.at[i, some], down_sem.at[i, q])
                for i, src in enumerate((do_hbm, dx_hbm))
            ]
        )

    def begin(k):
        for copy in stages[k]:
            copy.start()

    def arrive(k):
        for copy in stages[k]:
            copy.wait()
        if k + parts < len(stages):
            begin(k + parts)

    for k in range(parts):
        begin(k)

    sums = jnp.zeros((total, 4 * units), F32)
    squares = jnp.zeros((total, 128), F32)
    half = rows // 2
    low = lax.broadcasted_iota(jnp.int32, (groups, half, 128), 2) < 64
    for q in range(parts):
        arrive(q)

        def weights(at, size):
            return jnp.concatenate([wide[i, pl.ds(at, size), :] for i in range(4)], axis=1)

        tiles, stacks = [], []
        for b in range(q * quarter, (q + 1) * quarter):
            own = pl.multiple_of(2 * cols * b + cols * core, 32)
            oth = pl.multiple_of(2 * cols * b + cols * (1 - core), 32)
            tiles += [x_buf[:, b, i * rows : (i + 1) * rows, :].reshape(total, 128) for i in range(3)]
            stacks += [
                weights(own, 128),
                weights(oth, 128),
                weights(pl.multiple_of(own + 128, 32), cols - 128),
                weights(pl.multiple_of(oth + 128, 32), 256 - cols),
            ]
        for b in range(q * quarter, (q + 1) * quarter, 2):
            first, second = (x_buf[:, b + i, 3 * rows :, :].astype(F32) for i in range(2))
            top = jnp.where(low, first, second)
            bottom = jnp.where(low, second, first)
            bottom = pltpu.roll(bottom.reshape(groups * half, 128), 64, 1).reshape(groups, half, 128)
            tiles.append(jnp.concatenate([top, bottom], axis=1).reshape(total, 128).astype(BF16))
            for i in range(2):
                oth = pl.multiple_of(2 * cols * (b + i) + cols * (1 - core) + (384 - cols), 32)
                stacks.append(weights(oth, 2 * cols - 384))
        x = jnp.concatenate(tiles, axis=1)
        sums += jnp.dot(x, jnp.concatenate(stacks, axis=0), preferred_element_type=F32)
        for i, tile in enumerate(tiles):
            res = tile.astype(F32) * ig_ref[q * len(tiles) + i : q * len(tiles) + i + 1, :]
            squares += res * res

    scale = lax.rsqrt(jnp.sum(squares, axis=1, keepdims=True) / width + EPS)
    gate = sums[:, : 2 * units] * scale
    up = sums[:, 2 * units :] * scale
    act = (gate / (1.0 + jnp.exp(-gate)) * up).astype(BF16)

    for b in range(spans):
        if b % (spans // parts) == 0:
            arrive(parts + b // (spans // parts))
        some = slice(b * span, (b + 1) * span)
        w = jnp.concatenate([down[0, some, :], down[1, some, :]], axis=1)
        held[b] = lax.dot_general(act, w, NT, preferred_element_type=F32).astype(BF16)

    r = lax.broadcasted_iota(jnp.int32, (128, 128), 0)
    c = lax.broadcasted_iota(jnp.int32, (128, 128), 1)
    peer, piece, slot = r // 16, (r // 2) % spans, r % 2
    order = jnp.where(c == piece * 16 + peer * 2 + slot, 1.0, 0.0).astype(BF16)
    outs = []
    for g in range(total // 16):
        stack = jnp.concatenate([held[b, g * 16 : (g + 1) * 16, :] for b in range(spans)], axis=0)
        moved = jnp.dot(order, stack, preferred_element_type=F32).astype(BF16)
        some = pl.ds(g * 8, 8)
        out_buf[g * 8 : (g + 1) * 8] = moved.reshape(8, 16, span)
        outs.append(pltpu.make_async_copy(out_buf.at[some], out_hbm.at[some], out_sem.at[g]))
        outs[-1].start()
    for out in outs:
        out.wait()


def feed_forward(blocks, gate, up, down, inverse_gain, chips):
    peers, packed, _ = blocks.shape
    groups = peers // chips
    width, units = gate[0].shape
    cols = width // chips // 2
    rows = packed * 128 // (2 * cols)
    total = groups * rows
    spans, parts = 8, 4
    span = width // spans
    hbm = pl.BlockSpec(memory_space=pl.ANY)
    return pl.pallas_call(
        functools.partial(ffn_kernel, chips, cols, width),
        in_specs=[hbm] * 7
        + [pl.BlockSpec(memory_space=pltpu.VMEM)],
        out_specs=hbm,
        out_shape=pltpu.HBM((peers, 16, span), BF16),
        scratch_shapes=[
            pltpu.VMEM((groups, chips, packed, 128), BF16),
            pltpu.VMEM((4, width, units), BF16),
            pltpu.VMEM((2, width, units), BF16),
            pltpu.VMEM((spans, total, span), BF16),
            pltpu.VMEM((peers, 16, span), BF16),
            pltpu.SemaphoreType.DMA((parts,)),
            pltpu.SemaphoreType.DMA((4, parts)),
            pltpu.SemaphoreType.DMA((2, parts)),
            pltpu.SemaphoreType.DMA((total // 16,)),
        ],
        compiler_params=pltpu.CompilerParams(vmem_limit_bytes=VMEM),
        cost_estimate=pl.CostEstimate(
            flops=12 * total * units * width, bytes_accessed=14 * width * units, transcendentals=0
        ),
    )(
        blocks.reshape(groups, chips, packed, 128),
        *[in_hbm(v) for v in (*gate, *up, *down)],
        inverse_gain,
    )


def final_kernel(lengths_ref, parts_hbm, res_hbm, out_ref, parts, res, res_sem, sems):
    quarter = parts.shape[0] // 4
    copies = []
    for q in range(4):
        some = pl.ds(q * quarter, quarter)
        copies.append(pltpu.make_async_copy(parts_hbm.at[some], parts.at[some], sems.at[q]))
        copies[q].start()
    copy = pltpu.make_async_copy(res_hbm, res, res_sem)
    copy.start()
    copy.wait()
    total = res[...]
    for q in range(4):
        copies[q].wait()
        for p in range(q * quarter, (q + 1) * quarter):
            total += parts[p].astype(F32)
    row = lax.broadcasted_iota(jnp.int32, total.shape, 0)
    live = jnp.where(row % 2 == 0, lengths_ref[0], lengths_ref[1]) > 0
    total = jnp.where(live, total, 0.0)
    span = total.shape[1]
    for b in range(total.shape[0] // 2):
        out_ref[:, b * span : (b + 1) * span] = total[2 * b : 2 * b + 2].astype(BF16)


def finish(lengths, parts, res):
    vmem = pl.BlockSpec(memory_space=pltpu.VMEM)
    return pl.pallas_call(
        final_kernel,
        in_specs=[pl.BlockSpec(memory_space=pltpu.SMEM)] + [pl.BlockSpec(memory_space=pl.ANY)] * 2,
        out_specs=vmem,
        out_shape=jax.ShapeDtypeStruct((2, res.size // 2), BF16),
        scratch_shapes=[
            pltpu.VMEM(parts.shape, BF16),
            pltpu.VMEM(res.shape, F32),
            pltpu.SemaphoreType.DMA,
            pltpu.SemaphoreType.DMA((4,)),
        ],
        compiler_params=pltpu.CompilerParams(vmem_limit_bytes=16 * 2**20),
    )(lengths, parts, res)


def make_shards(groups, devs):
    chips = devs // 2
    peers = groups * chips
    plane = [[2 * k + c for k in range(chips)] for c in range(2)]
    cube = [[2 * k + c for k in range(peers)] for c in range(2)]
    other = [(i, i ^ 1) for i in range(devs)]

    def shards(
        query,
        key_cache,
        value_cache,
        lengths,
        hidden,
        out_weight,
        ffn_gain,
        gate_weight,
        up_weight,
        down_weight,
    ):
        me = lax.axis_index("dev")
        core = lax.rem(me, 2)
        chip = lax.div(me, 2)
        slots, width = hidden.shape
        cols = width // devs

        def swap(w):
            return lax.ppermute(w, "dev", other)

        out_own = out_weight.T
        out_oth = swap(out_own)
        message = attend(lengths, query, key_cache, value_cache, hidden, chips)
        got = lax.all_to_all(message, "dev", 0, 0, axis_index_groups=plane)
        block = project(got, ffn_gain.reshape(width // 128, 128), out_own, out_oth, peers)
        blocks = lax.all_to_all(block, ("grp", "dev"), 0, 0, axis_index_groups=cube)

        gate_weight, up_weight, down_weight, gains, _ = lax.optimization_barrier(
            (gate_weight, up_weight, down_weight, ffn_gain, block)
        )
        gate_oth = swap(gate_weight)
        up_oth = swap(up_weight)
        down_oth = swap(down_weight)
        inv = 1.0 / gains.reshape(chips, 2, cols)
        inv = jnp.where(core == 0, inv, inv[:, ::-1])
        inv = jnp.concatenate(
            [
                jnp.stack(
                    [
                        inv[:, 0, :128],
                        inv[:, 1, :128],
                        jnp.concatenate([inv[:, 0, 128:cols], inv[:, 1, 128 : 384 - cols]], axis=1),
                    ],
                    axis=1,
                ).reshape(chips // 4, 12, 128),
                inv[:, 1, 384 - cols : cols].reshape(chips // 4, 2, 128),
            ],
            axis=1,
        ).reshape(width // 128, 128)
        partial = feed_forward(
            blocks,
            (gate_weight, gate_oth),
            (up_weight, up_oth),
            (down_weight, down_oth),
            inv,
            chips,
        )
        parts = lax.all_to_all(partial, ("grp", "dev"), 0, 0, axis_index_groups=cube)

        rows = chips * slots
        mine = lax.dynamic_slice(
            blocks, (lax.axis_index("grp") * chips, 0, 0), (chips,) + blocks.shape[1:]
        )
        full = lax.dynamic_slice(
            mine[:, : 3 * rows].reshape(chips, 3, rows, 128), (0, 0, chip * slots, 0), (chips, 3, slots, 128)
        )
        last = mine[:, 3 * rows :].reshape(chips // 2, 2, rows // 2, 2, 64)
        last = jnp.stack([last[:, 0], last[:, 1, :, ::-1]], axis=1)
        last = last.transpose(0, 1, 3, 2, 4).reshape(chips, rows, 64)
        last = lax.dynamic_slice(last, (0, chip * slots, 0), (chips, slots, 64))
        own = jnp.concatenate([full[:, 0], full[:, 2, :, : cols - 128]], axis=2)
        oth = jnp.concatenate([full[:, 1], full[:, 2, :, cols - 128 :], last], axis=2)
        mine = jnp.stack([jnp.where(core == 0, own, oth), jnp.where(core == 0, oth, own)], axis=2)
        mine = mine.astype(F32).transpose(1, 0, 2, 3).reshape(slots, width) / ffn_gain
        spans = 16 // slots
        mine = mine.reshape(slots, spans, width // spans).transpose(1, 0, 2).reshape(16, width // spans)
        return finish(lengths, parts, mine)

    return shards


def solution(mesh):
    both = ("grp", "dev")
    in_specs = (
        P(both, None),
        P(both, None, None),
        P(both, None, None),
        P(both),
        P(both, None),
        P(None, "dev"),
        P(),
        P(None, both),
        P(None, both),
        P(None, both),
    )
    body = make_shards(mesh.shape["grp"], mesh.shape["dev"])
    return jax.shard_map(body, mesh=mesh, in_specs=in_specs, out_specs=P(both, None), check_vma=False)
```

```python
import functools

import jax
import jax.numpy as jnp
from jax import lax
from jax.experimental import pallas as pl
from jax.experimental.pallas import tpu as pltpu
from jax.sharding import PartitionSpec as P

BF16 = jnp.bfloat16
F32 = jnp.float32
EPS = 1e-05
VMEM = 32 * 2**20
HOPS = 4
NT = (((1,), (1,)), ((), ()))


def attend_kernel(lengths_ref, q_hbm, k_hbm, v_hbm, hid_hbm, token_hbm, out_ref, q_ref, hid_ref, keys, values, small_sems, sems):
    slots, span, dim = keys.shape
    heads = q_ref.shape[1] // dim
    chips = out_ref.shape[0]
    small = [
        pltpu.make_async_copy(src, dst, small_sems.at[i])
        for i, (src, dst) in enumerate(((q_hbm, q_ref), (hid_hbm, hid_ref)))
    ]
    for copy in small:
        copy.start()
    copies = []
    for i, (src, dst) in enumerate(((k_hbm, keys), (v_hbm, values))):
        for s in range(slots):
            copy = pltpu.make_async_copy(src.at[s], dst.at[s], sems.at[i, s])
            copy.start()
            copies.append(copy)
    small[0].wait()
    q = q_ref[...].astype(F32)
    q = jnp.concatenate(
        [q[s : s + 1, h * dim : (h + 1) * dim] for s in range(slots) for h in range(heads)], axis=0
    ).astype(BF16)
    small[1].wait()
    hid = hid_ref[...].astype(F32)
    row = lax.broadcasted_iota(jnp.int32, (16, 128), 0)
    tiles = [
        jnp.where(row % slots == 0, hid[0:1, t * 128 : (t + 1) * 128], hid[1:2, t * 128 : (t + 1) * 128])
        for t in range(hid.shape[1] // 128)
    ]
    extra = []
    for p in range(chips):
        first = (p * hid.shape[1] // chips) // 128
        held = jnp.zeros((16, 128), F32)
        for i in range(4):
            held = jnp.where(row // slots == i, tiles[first + i], held)
        extra.append(held.astype(BF16))
    parts = []
    position = lax.broadcasted_iota(jnp.int32, (heads, span), 1)
    for s in range(slots):
        copies[s].wait()
        scores = lax.dot_general(
            q[s * heads : (s + 1) * heads, :], keys[s], NT, preferred_element_type=F32
        ) * dim ** (-0.5)
        scores = jnp.where(position < jnp.maximum(lengths_ref[s], 1), scores, -jnp.inf)
        weights = jnp.exp(scores - jnp.max(scores, axis=1, keepdims=True))
        parts.append((weights * (1.0 / jnp.sum(weights, axis=1, keepdims=True))).astype(BF16))
    for s in range(slots):
        copies[slots + s].wait()
        parts[s] = jnp.dot(parts[s], values[s], preferred_element_type=F32).astype(BF16)
    both = jnp.concatenate(parts, axis=0)
    pieces = 16 // slots
    per = heads // pieces
    r = lax.broadcasted_iota(jnp.int32, (16, slots * heads), 0)
    c = lax.broadcasted_iota(jnp.int32, (16, slots * heads), 1)
    rows = []
    for j in range(per):
        take = jnp.where(c == (r % slots) * heads + (r // slots) * per + j, 1.0, 0.0).astype(BF16)
        rows.append(jnp.dot(take, both, preferred_element_type=F32).astype(BF16))
    rows = jnp.concatenate(rows, axis=1)
    for p in range(chips):
        out_ref[p] = jnp.concatenate([rows, extra[p]], axis=1)


def attend(lengths, query, key_cache, value_cache, hidden, token, chips):
    slots, span, dim = key_cache.shape
    hbm = pl.BlockSpec(memory_space=pl.ANY)
    vmem = pl.BlockSpec(memory_space=pltpu.VMEM)
    lanes = query.shape[1] * slots // 16 + 128
    return pl.pallas_call(
        attend_kernel,
        in_specs=[pl.BlockSpec(memory_space=pltpu.SMEM)] + [hbm] * 5,
        out_specs=vmem,
        out_shape=pltpu.HBM((chips, 16, lanes), BF16),
        scratch_shapes=[
            pltpu.VMEM(query.shape, BF16),
            pltpu.VMEM(hidden.shape, BF16),
            pltpu.VMEM(key_cache.shape, BF16),
            pltpu.VMEM(value_cache.shape, BF16),
            pltpu.SemaphoreType.DMA((2,)),
            pltpu.SemaphoreType.DMA((2, slots)),
        ],
        compiler_params=pltpu.CompilerParams(vmem_limit_bytes=12 * 2**20),
    )(in_hbm(lengths), *[in_hbm(v) for v in (query, key_cache, value_cache, hidden)], token)


def project_kernel(
    steps, cols, x_ref, own_ref, oth_ref, gain_ref, *refs
):
    _, _, _, out_hbm, res_ref, x_rows, hid_rows, acc_own, acc_oth, block, out_sem = refs
    step = pl.program_id(0)
    chips, deep, lanes = x_ref.shape
    chunk = own_ref.shape[1]
    slots = 2
    pieces = deep // slots
    rows = chips * slots
    wide = x_rows.shape[1] // pieces

    @pl.when(step == 0)
    def _():
        r = lax.broadcasted_iota(jnp.int32, (chips * deep, chips * deep), 0)
        c = lax.broadcasted_iota(jnp.int32, (chips * deep, chips * deep), 1)
        order = c == (r % rows) // slots * deep + r // rows * slots + r % slots
        order = jnp.where(order, 1.0, 0.0).astype(BF16)
        x = jnp.dot(order, x_ref[...].reshape(chips * deep, lanes), preferred_element_type=F32)
        for i in range(pieces):
            x_rows[:, i * wide : (i + 1) * wide] = x[i * rows : (i + 1) * rows, :wide].astype(BF16)
        for i in range(4):
            hid_rows[i] = x[i * rows : (i + 1) * rows, wide:]

    x = x_rows[:, pl.ds(pl.multiple_of(step * chunk, chunk), chunk)]
    for acc, w in ((acc_own, own_ref), (acc_oth, oth_ref)):
        part = lax.dot_general(x, w[...], NT, preferred_element_type=F32)

        @pl.when(step == 0)
        def _():
            acc[...] = part

        @pl.when(step > 0)
        def _():
            acc[...] += part

    @pl.when(step == steps - 1)
    def _():
        me = lax.axis_index("dev")
        core, chip = me % 2, me // 2
        lane = lax.broadcasted_iota(jnp.int32, (rows, 128), 1)

        def ahead(tiles, shift):
            moved = [pltpu.roll(t, 128 - shift, 1) for t in tiles]
            return [jnp.where(lane < 128 - shift, a, b) for a, b in zip(moved, moved[1:] + moved[-1:])]

        def halves(tiles):
            tiles = [jnp.where(chip % 2 == 0, a, b) for a, b in zip(tiles, ahead(tiles, 64))]
            first = jnp.concatenate(tiles[:2], axis=1)
            second = jnp.concatenate(ahead(tiles[1:], cols - 128)[:2], axis=1)
            return jnp.where(core == 0, first, second), jnp.where(core == 0, second, first)

        hids = halves([hid_rows[i] for i in range(4)])
        start = 7 * (chip // 2) + 3 * (chip % 2)
        gains = halves([jnp.broadcast_to(gain_ref[pl.ds(start + i, 1), :], (rows, 128)) for i in range(4)])
        pad = jnp.zeros((rows, 256 - cols), F32)
        held, sent = [], []
        for acc, hid, gain in zip((acc_own, acc_oth), hids, gains):
            projected = jnp.concatenate([acc[...].astype(BF16).astype(F32), pad], axis=1)
            held.append(hid + projected)
            sent.append(held[-1] * gain)

        first = jnp.where(core == 0, held[0], held[1])
        second = jnp.where(core == 0, held[1], held[0])
        near, far = pltpu.roll(second[:, :128], cols - 128, 1), pltpu.roll(second[:, 128:], cols - 128, 1)
        tiles = [
            first[:, :128],
            jnp.where(lane < cols - 128, first[:, 128:], near),
            jnp.where(lane < cols - 128, near, far),
            jnp.where(lane < 64, far, 0.0),
        ]
        moved = [pltpu.roll(t, 64, 1) for t in tiles]
        for i in range(4):
            before = moved[i - 1] if i else jnp.zeros((rows, 128), F32)
            res_ref[i] = jnp.where(chip % 2 == 0, tiles[i], jnp.where(lane < 64, before, moved[i]))
        own_tail, oth_tail = sent[0][:, 128:], sent[1][:, 128:]
        third = jnp.where(lane < cols - 128, own_tail, pltpu.roll(oth_tail, cols - 128, 1))
        rest = pltpu.roll(oth_tail, 128 - (256 - cols), 1)
        turned = pltpu.roll(rest, 64, 1)
        half = rows // 2
        low = lax.broadcasted_iota(jnp.int32, (half, 128), 1) < 64
        even = jnp.where(low, rest[:half], turned[half:])
        odd = jnp.where(low, rest[half:], turned[:half])
        last = jnp.where(chip % 2 == 0, even, odd)
        packed = jnp.concatenate([sent[0][:, :128], sent[1][:, :128], third, last], axis=0).astype(BF16)
        copies = block.shape[0]
        for p in range(copies):
            block[p] = packed
        outs = []
        for p in range(out_hbm.shape[0] // copies):
            out = pltpu.make_async_copy(block, out_hbm.at[pl.ds(p * copies, copies)], out_sem.at[p])
            out.start()
            outs.append(out)
        for out in outs:
            out.wait()


def in_hbm(v):
    return pltpu.with_memory_space_constraint(v, pltpu.HBM)


def project(messages, gain, out_own, out_oth, arrived, peers):
    cols, depth = out_own.shape
    rows = messages.shape[0] * 2
    packed = rows * 2 * cols // 128
    steps = 1
    chunk = depth // steps
    return pl.pallas_call(
        functools.partial(project_kernel, steps, cols),
        grid=(steps,),
        in_specs=[
            pl.BlockSpec(messages.shape, lambda k: (0, 0, 0)),
            pl.BlockSpec((cols, chunk), lambda k: (0, k)),
            pl.BlockSpec((cols, chunk), lambda k: (0, k)),
            pl.BlockSpec(gain.shape, lambda k: (0, 0)),
        ]
        + [pl.BlockSpec(memory_space=pl.ANY)] * 3,
        out_specs=[
            pl.BlockSpec(memory_space=pl.ANY),
            pl.BlockSpec((4, rows, 128), lambda k: (0, 0, 0)),
        ],
        out_shape=[pltpu.HBM((peers, packed, 128), BF16), pltpu.HBM((4, rows, 128), F32)],
        scratch_shapes=[
            pltpu.VMEM((rows, depth), BF16),
            pltpu.VMEM((4, rows, 128), F32),
            pltpu.VMEM((rows, cols), F32),
            pltpu.VMEM((rows, cols), F32),
            pltpu.VMEM((8, packed, 128), BF16),
            pltpu.SemaphoreType.DMA((peers // 8,)),
        ],
        compiler_params=pltpu.CompilerParams(vmem_limit_bytes=24 * 2**20),
        cost_estimate=pl.CostEstimate(
            flops=4 * rows * cols * depth, bytes_accessed=4 * cols * depth, transcendentals=0
        ),
    )(messages, out_own, out_oth, in_hbm(gain), *arrived)


def ffn_kernel(
    chips, cols, width,
    x_buf, go_ref, gx_ref, uo_ref, ux_ref, do_ref, dx_ref, gain_ref, res_ref, out_hbm, held, out_buf, out_sem,
):
    groups, _, packed, _ = x_buf.shape
    rows = packed * 128 // (2 * cols)
    total = groups * rows
    units = go_ref.shape[1]
    quarter = 4
    parts = chips // quarter
    me = lax.axis_index("dev")
    core, chip = me % 2, me // 2
    spans, span = 8, width // 8
    per = span // 128
    sums = jnp.zeros((total, 4 * units), F32)
    squares = jnp.zeros((total, 128), F32)
    half = rows // 2
    low = lax.broadcasted_iota(jnp.int32, (groups, half, 128), 2) < 64
    lane = lax.broadcasted_iota(jnp.int32, (1, 128), 1)

    def ahead(tiles, shift):
        moved = [pltpu.roll(t, 128 - shift, 1) for t in tiles]
        return [jnp.where(lane < 128 - shift, a, b) for a, b in zip(moved, moved[1:] + moved[-1:])]

    def inverse(b):
        start = 7 * (b // 2) + 3 * (b % 2)
        tiles = [gain_ref[start + i : start + i + 1, :] for i in range(4)]
        if b % 2:
            tiles = ahead(tiles, 64)
        first, last = tiles[:2], ahead(tiles[1:], cols - 128)[:2]
        own = [jnp.where(core == 0, p, q) for p, q in zip(first, last)]
        oth = [jnp.where(core == 0, q, p) for p, q in zip(first, last)]
        third = jnp.where(lane < cols - 128, own[1], pltpu.roll(oth[1], cols - 128, 1))
        return [1.0 / own[0], 1.0 / oth[0], 1.0 / third], pltpu.roll(oth[1], 128 - (256 - cols), 1)

    for q in range(parts):

        def weights(at, size):
            return jnp.concatenate([w[pl.ds(at, size), :] for w in (go_ref, gx_ref, uo_ref, ux_ref)], axis=1)

        tiles, stacks, inverses, rests = [], [], [], {}
        for b in range(q * quarter, (q + 1) * quarter):
            own = pl.multiple_of(2 * cols * b + cols * core, 32)
            oth = pl.multiple_of(2 * cols * b + cols * (1 - core), 32)
            tiles += [x_buf[:, b, i * rows : (i + 1) * rows, :].reshape(total, 128) for i in range(3)]
            stacks += [
                weights(own, 128),
                weights(oth, 128),
                weights(pl.multiple_of(own + 128, 32), cols - 128),
                weights(pl.multiple_of(oth + 128, 32), 256 - cols),
            ]
            inv, rests[b] = inverse(b)
            inverses += inv
        for b in range(q * quarter, (q + 1) * quarter, 2):
            first, second = (x_buf[:, b + i, 3 * rows :, :].astype(F32) for i in range(2))
            top = jnp.where(low, first, second)
            bottom = jnp.where(low, second, first)
            bottom = pltpu.roll(bottom.reshape(groups * half, 128), 64, 1).reshape(groups, half, 128)
            tiles.append(jnp.concatenate([top, bottom], axis=1).reshape(total, 128).astype(BF16))
            inverses.append(1.0 / jnp.where(lane < 64, rests[b], pltpu.roll(rests[b + 1], 64, 1)))
            for i in range(2):
                oth = pl.multiple_of(2 * cols * (b + i) + cols * (1 - core) + (384 - cols), 32)
                stacks.append(weights(oth, 2 * cols - 384))
        x = jnp.concatenate(tiles, axis=1)
        sums += jnp.dot(x, jnp.concatenate(stacks, axis=0), preferred_element_type=F32)
        for tile, inv in zip(tiles, inverses):
            res = tile.astype(F32) * inv
            squares += res * res

    scale = lax.rsqrt(jnp.sum(squares, axis=1, keepdims=True) / width + EPS)
    gate = sums[:, : 2 * units] * scale
    up = sums[:, 2 * units :] * scale
    act = (gate / (1.0 + jnp.exp(-gate)) * up).astype(BF16)

    for b in range(spans):
        some = slice(b * span, (b + 1) * span)
        w = jnp.concatenate([do_ref[some, :], dx_ref[some, :]], axis=1)
        product = lax.dot_general(act, w, NT, preferred_element_type=F32).astype(BF16)
        for t in range(per):
            held[b * per + t] = product[:, t * 128 : (t + 1) * 128]
    mine = pl.multiple_of(rows * lax.axis_index("grp"), rows)
    start = 7 * (chip // 2) + 3 * (chip % 2)
    for i in range(4):
        at = (pl.ds(start + i, 1), pl.ds(mine, rows))
        held[at] = (held[at].astype(F32) + res_ref[i : i + 1]).astype(BF16)

    r = lax.broadcasted_iota(jnp.int32, (128, 128), 0)
    c = lax.broadcasted_iota(jnp.int32, (128, 128), 1)
    peer, piece, slot = r // 16, (r // 2) % spans, r % 2
    order = jnp.where(c == piece * 16 + peer * 2 + slot, 1.0, 0.0).astype(BF16)
    outs = []
    for g in range(total // 16):
        stack = jnp.concatenate(
            [
                jnp.concatenate([held[b * per + t, g * 16 : (g + 1) * 16, :] for t in range(per)], axis=1)
                for b in range(spans)
            ],
            axis=0,
        )
        moved = jnp.dot(order, stack, preferred_element_type=F32).astype(BF16)
        some = pl.ds(g * 8, 8)
        out_buf[g * 8 : (g + 1) * 8] = moved.reshape(8, 16, span)
        outs.append(pltpu.make_async_copy(out_buf.at[some], out_hbm.at[some], out_sem.at[g]))
        outs[-1].start()
    for out in outs:
        out.wait()


def feed_forward(blocks, gate, up, down, gain, residual, chips):
    peers, packed, _ = blocks.shape
    groups = peers // chips
    width, units = gate[0].shape
    cols = width // chips // 2
    rows = packed * 128 // (2 * cols)
    total = groups * rows
    spans = 8
    span = width // spans
    vmem = pl.BlockSpec(memory_space=pltpu.VMEM)
    return pl.pallas_call(
        functools.partial(ffn_kernel, chips, cols, width),
        in_specs=[vmem] * 9,
        out_specs=pl.BlockSpec(memory_space=pl.ANY),
        out_shape=pltpu.HBM((peers, 16, span), BF16),
        scratch_shapes=[
            pltpu.VMEM((width // 128, total, 128), BF16),
            pltpu.VMEM((peers, 16, span), BF16),
            pltpu.SemaphoreType.DMA((total // 16,)),
        ],
        compiler_params=pltpu.CompilerParams(vmem_limit_bytes=28 * 2**20),
        cost_estimate=pl.CostEstimate(
            flops=12 * total * units * width, bytes_accessed=14 * width * units, transcendentals=0
        ),
    )(
        blocks.reshape(groups, chips, packed, 128),
        *gate,
        *up,
        *down,
        gain,
        residual,
    )


def final_kernel(lengths_ref, parts_hbm, out_ref, parts, sems):
    quarter = parts.shape[0] // 4
    copies = []
    for q in range(4):
        some = pl.ds(q * quarter, quarter)
        copies.append(pltpu.make_async_copy(parts_hbm.at[some], parts.at[some], sems.at[q]))
        copies[q].start()
    total = jnp.zeros(parts.shape[1:], F32)
    for q in range(4):
        copies[q].wait()
        for p in range(q * quarter, (q + 1) * quarter):
            total += parts[p].astype(F32)
    row = lax.broadcasted_iota(jnp.int32, total.shape, 0)
    live = jnp.where(row % 2 == 0, lengths_ref[0], lengths_ref[1]) > 0
    total = jnp.where(live, total, 0.0)
    span = total.shape[1]
    for b in range(total.shape[0] // 2):
        out_ref[:, b * span : (b + 1) * span] = total[2 * b : 2 * b + 2].astype(BF16)


def finish(lengths, parts):
    _, rows, span = parts.shape
    return pl.pallas_call(
        final_kernel,
        in_specs=[pl.BlockSpec(memory_space=pltpu.SMEM), pl.BlockSpec(memory_space=pl.ANY)],
        out_specs=pl.BlockSpec(memory_space=pltpu.VMEM),
        out_shape=jax.ShapeDtypeStruct((2, rows * span // 2), BF16),
        scratch_shapes=[pltpu.VMEM(parts.shape, BF16), pltpu.SemaphoreType.DMA((4,))],
        compiler_params=pltpu.CompilerParams(vmem_limit_bytes=16 * 2**20),
    )(in_hbm(lengths), parts)


def make_shards(groups, devs):
    chips = devs // 2
    peers = groups * chips
    plane = [[2 * k + c for k in range(chips)] for c in range(2)]
    cube = [[2 * k + c for k in range(peers)] for c in range(2)]
    other = [(i, i ^ 1) for i in range(devs)]
    links = [[(i, i ^ 2) for i in range(1, devs, 2)]] * HOPS

    def shards(
        query,
        key_cache,
        value_cache,
        lengths,
        hidden,
        out_weight,
        ffn_gain,
        gate_weight,
        up_weight,
        down_weight,
    ):
        slots, width = hidden.shape

        def swap(w):
            return lax.ppermute(w, "dev", other)

        out_own = out_weight.T
        out_oth = swap(out_own)
        gate = (gate_weight, swap(gate_weight))
        up = (up_weight, swap(up_weight))
        down = (down_weight, swap(down_weight))
        token = lengths
        for link in links:
            token = lax.ppermute(token, "dev", link)
        message = attend(lengths, query, key_cache, value_cache, hidden, token, chips)
        got = lax.all_to_all(message, "dev", 0, 0, axis_index_groups=plane)
        gain = ffn_gain.reshape(width // 128, 128)
        block, residual = project(got, gain, out_own, out_oth, (gate[1], up[1], down[1]), peers)

        both = ("grp", "dev")
        blocks = lax.all_to_all(block, both, 0, 0, axis_index_groups=cube)
        partial = feed_forward(blocks, gate, up, down, gain, residual, chips)
        parts = lax.all_to_all(partial, both, 0, 0, axis_index_groups=cube)
        return finish(lengths, parts)

    return shards


def solution(mesh):
    both = ("grp", "dev")
    in_specs = (
        P(both, None),
        P(both, None, None),
        P(both, None, None),
        P(both),
        P(both, None),
        P(None, "dev"),
        P(),
        P(None, both),
        P(None, both),
        P(None, both),
    )
    body = make_shards(mesh.shape["grp"], mesh.shape["dev"])
    return jax.shard_map(body, mesh=mesh, in_specs=in_specs, out_specs=P(both, None), check_vma=False)
```

```python
import functools

import jax
import jax.numpy as jnp
from jax import lax
from jax.experimental import pallas as pl
from jax.experimental.pallas import tpu as pltpu
from jax.sharding import PartitionSpec as P

BF16 = jnp.bfloat16
F32 = jnp.float32
EPS = 1e-05
VMEM = 32 * 2**20
NT = (((1,), (1,)), ((), ()))


def attend_kernel(lengths_ref, q_hbm, k_hbm, v_hbm, hid_hbm, token_hbm, out_ref, q_ref, hid_ref, keys, values, small_sems, sems):
    slots, span, dim = keys.shape
    heads = q_ref.shape[1] // dim
    chips = out_ref.shape[0]
    small = [
        pltpu.make_async_copy(src, dst, small_sems.at[i])
        for i, (src, dst) in enumerate(((q_hbm, q_ref), (hid_hbm, hid_ref)))
    ]
    for copy in small:
        copy.start()
    copies = []
    for i, (src, dst) in enumerate(((k_hbm, keys), (v_hbm, values))):
        for s in range(slots):
            copy = pltpu.make_async_copy(src.at[s], dst.at[s], sems.at[i, s])
            copy.start()
            copies.append(copy)
    small[0].wait()
    q = q_ref[...].astype(F32)
    q = jnp.concatenate(
        [q[s : s + 1, h * dim : (h + 1) * dim] for s in range(slots) for h in range(heads)], axis=0
    ).astype(BF16)
    small[1].wait()
    hid = hid_ref[...].astype(F32)
    row = lax.broadcasted_iota(jnp.int32, (16, 128), 0)
    tiles = [
        jnp.where(row % slots == 0, hid[0:1, t * 128 : (t + 1) * 128], hid[1:2, t * 128 : (t + 1) * 128])
        for t in range(hid.shape[1] // 128)
    ]
    extra = []
    for p in range(chips):
        first = (p * hid.shape[1] // chips) // 128
        held = jnp.zeros((16, 128), F32)
        for i in range(4):
            held = jnp.where(row // slots == i, tiles[first + i], held)
        extra.append(held.astype(BF16))
    parts = []
    position = lax.broadcasted_iota(jnp.int32, (heads, span), 1)
    for copy in copies[:slots]:
        copy.wait()
    for s in range(slots):
        scores = lax.dot_general(
            q[s * heads : (s + 1) * heads, :], keys[s], NT, preferred_element_type=F32
        ) * dim ** (-0.5)
        scores = jnp.where(position < jnp.maximum(lengths_ref[s], 1), scores, -jnp.inf)
        weights = jnp.exp(scores - jnp.max(scores, axis=1, keepdims=True))
        parts.append((weights * (1.0 / jnp.sum(weights, axis=1, keepdims=True))).astype(BF16))
    for copy in copies[slots:]:
        copy.wait()
    for s in range(slots):
        parts[s] = jnp.dot(parts[s], values[s], preferred_element_type=F32).astype(BF16)
    both = jnp.concatenate(parts, axis=0)
    pieces = 16 // slots
    per = heads // pieces
    r = lax.broadcasted_iota(jnp.int32, (16, slots * heads), 0)
    c = lax.broadcasted_iota(jnp.int32, (16, slots * heads), 1)
    rows = []
    for j in range(per):
        take = jnp.where(c == (r % slots) * heads + (r // slots) * per + j, 1.0, 0.0).astype(BF16)
        rows.append(jnp.dot(take, both, preferred_element_type=F32).astype(BF16))
    rows = jnp.concatenate(rows, axis=1)
    for p in range(chips):
        out_ref[p] = jnp.concatenate([rows, extra[p]], axis=1)


def attend(lengths, query, key_cache, value_cache, hidden, token, chips):
    slots, span, dim = key_cache.shape
    hbm = pl.BlockSpec(memory_space=pl.ANY)
    vmem = pl.BlockSpec(memory_space=pltpu.VMEM)
    lanes = query.shape[1] * slots // 16 + 128
    return pl.pallas_call(
        attend_kernel,
        in_specs=[pl.BlockSpec(memory_space=pltpu.SMEM)] + [hbm] * 5,
        out_specs=vmem,
        out_shape=pltpu.HBM((chips, 16, lanes), BF16),
        scratch_shapes=[
            pltpu.VMEM(query.shape, BF16),
            pltpu.VMEM(hidden.shape, BF16),
            pltpu.VMEM(key_cache.shape, BF16),
            pltpu.VMEM(value_cache.shape, BF16),
            pltpu.SemaphoreType.DMA((2,)),
            pltpu.SemaphoreType.DMA((2, slots)),
        ],
        compiler_params=pltpu.CompilerParams(vmem_limit_bytes=12 * 2**20),
    )(in_hbm(lengths), *[in_hbm(v) for v in (query, key_cache, value_cache, hidden)], token)


def project_kernel(
    steps, cols, x_ref, own_ref, oth_ref, gain_ref, *refs
):
    _, _, _, out_hbm, res_ref, x_rows, hid_rows, acc_own, acc_oth, block, out_sem = refs
    step = pl.program_id(0)
    chips, deep, lanes = x_ref.shape
    chunk = own_ref.shape[1]
    slots = 2
    pieces = deep // slots
    rows = chips * slots
    wide = x_rows.shape[1] // pieces

    @pl.when(step == 0)
    def _():
        r = lax.broadcasted_iota(jnp.int32, (chips * deep, chips * deep), 0)
        c = lax.broadcasted_iota(jnp.int32, (chips * deep, chips * deep), 1)
        order = c == (r % rows) // slots * deep + r // rows * slots + r % slots
        order = jnp.where(order, 1.0, 0.0).astype(BF16)
        x = jnp.dot(order, x_ref[...].reshape(chips * deep, lanes), preferred_element_type=F32)
        for i in range(pieces):
            x_rows[:, i * wide : (i + 1) * wide] = x[i * rows : (i + 1) * rows, :wide].astype(BF16)
        for i in range(4):
            hid_rows[i] = x[i * rows : (i + 1) * rows, wide:]

    x = x_rows[:, pl.ds(pl.multiple_of(step * chunk, chunk), chunk)]
    for acc, w in ((acc_own, own_ref), (acc_oth, oth_ref)):
        part = lax.dot_general(x, w[...], NT, preferred_element_type=F32)

        @pl.when(step == 0)
        def _():
            acc[...] = part

        @pl.when(step > 0)
        def _():
            acc[...] += part

    @pl.when(step == steps - 1)
    def _():
        me = lax.axis_index("dev")
        core, chip = me % 2, me // 2
        lane = lax.broadcasted_iota(jnp.int32, (rows, 128), 1)

        def ahead(tiles, shift):
            moved = [pltpu.roll(t, 128 - shift, 1) for t in tiles]
            return [jnp.where(lane < 128 - shift, a, b) for a, b in zip(moved, moved[1:] + moved[-1:])]

        def halves(tiles):
            tiles = [jnp.where(chip % 2 == 0, a, b) for a, b in zip(tiles, ahead(tiles, 64))]
            first = jnp.concatenate(tiles[:2], axis=1)
            second = jnp.concatenate(ahead(tiles[1:], cols - 128)[:2], axis=1)
            return jnp.where(core == 0, first, second), jnp.where(core == 0, second, first)

        hids = halves([hid_rows[i] for i in range(4)])
        start = 7 * (chip // 2) + 3 * (chip % 2)
        gains = halves([jnp.broadcast_to(gain_ref[pl.ds(start + i, 1), :], (rows, 128)) for i in range(4)])
        pad = jnp.zeros((rows, 256 - cols), F32)
        held, sent = [], []
        for acc, hid, gain in zip((acc_own, acc_oth), hids, gains):
            projected = jnp.concatenate([acc[...].astype(BF16).astype(F32), pad], axis=1)
            held.append(hid + projected)
            sent.append(held[-1] * gain)

        first = jnp.where(core == 0, held[0], held[1])
        second = jnp.where(core == 0, held[1], held[0])
        near, far = pltpu.roll(second[:, :128], cols - 128, 1), pltpu.roll(second[:, 128:], cols - 128, 1)
        tiles = [
            first[:, :128],
            jnp.where(lane < cols - 128, first[:, 128:], near),
            jnp.where(lane < cols - 128, near, far),
            jnp.where(lane < 64, far, 0.0),
        ]
        moved = [pltpu.roll(t, 64, 1) for t in tiles]
        for i in range(4):
            before = moved[i - 1] if i else jnp.zeros((rows, 128), F32)
            res_ref[i] = jnp.where(chip % 2 == 0, tiles[i], jnp.where(lane < 64, before, moved[i]))
        own_tail, oth_tail = sent[0][:, 128:], sent[1][:, 128:]
        third = jnp.where(lane < cols - 128, own_tail, pltpu.roll(oth_tail, cols - 128, 1))
        rest = pltpu.roll(oth_tail, 128 - (256 - cols), 1)
        turned = pltpu.roll(rest, 64, 1)
        half = rows // 2
        low = lax.broadcasted_iota(jnp.int32, (half, 128), 1) < 64
        even = jnp.where(low, rest[:half], turned[half:])
        odd = jnp.where(low, rest[half:], turned[:half])
        last = jnp.where(chip % 2 == 0, even, odd)
        packed = jnp.concatenate([sent[0][:, :128], sent[1][:, :128], third, last], axis=0).astype(BF16)
        copies = block.shape[0]
        for p in range(copies):
            block[p] = packed
        outs = []
        for p in range(out_hbm.shape[0] // copies):
            out = pltpu.make_async_copy(block, out_hbm.at[pl.ds(p * copies, copies)], out_sem.at[p])
            out.start()
            outs.append(out)
        for out in outs:
            out.wait()


def in_hbm(v):
    return pltpu.with_memory_space_constraint(v, pltpu.HBM)


def project(messages, gain, out_own, out_oth, arrived, peers):
    cols, depth = out_own.shape
    rows = messages.shape[0] * 2
    packed = rows * 2 * cols // 128
    steps = 1
    chunk = depth // steps
    return pl.pallas_call(
        functools.partial(project_kernel, steps, cols),
        grid=(steps,),
        in_specs=[
            pl.BlockSpec(messages.shape, lambda k: (0, 0, 0)),
            pl.BlockSpec((cols, chunk), lambda k: (0, k)),
            pl.BlockSpec((cols, chunk), lambda k: (0, k)),
            pl.BlockSpec(gain.shape, lambda k: (0, 0)),
        ]
        + [pl.BlockSpec(memory_space=pl.ANY)] * 3,
        out_specs=[
            pl.BlockSpec(memory_space=pl.ANY),
            pl.BlockSpec((4, rows, 128), lambda k: (0, 0, 0)),
        ],
        out_shape=[pltpu.HBM((peers, packed, 128), BF16), pltpu.HBM((4, rows, 128), F32)],
        scratch_shapes=[
            pltpu.VMEM((rows, depth), BF16),
            pltpu.VMEM((4, rows, 128), F32),
            pltpu.VMEM((rows, cols), F32),
            pltpu.VMEM((rows, cols), F32),
            pltpu.VMEM((8, packed, 128), BF16),
            pltpu.SemaphoreType.DMA((peers // 8,)),
        ],
        compiler_params=pltpu.CompilerParams(vmem_limit_bytes=24 * 2**20),
        cost_estimate=pl.CostEstimate(
            flops=4 * rows * cols * depth, bytes_accessed=4 * cols * depth, transcendentals=0
        ),
    )(messages, out_own, out_oth, in_hbm(gain), *arrived)


def ffn_kernel(
    chips, cols, width,
    x_buf, go_ref, gx_ref, uo_ref, ux_ref, do_ref, dx_ref, gain_ref, res_hbm, out_hbm,
    held, out_buf, res_ref, res_sem, out_sem,
):
    groups, _, packed, _ = x_buf.shape
    rows = packed * 128 // (2 * cols)
    total = groups * rows
    units = go_ref.shape[1]
    quarter = 4
    parts = chips // quarter
    me = lax.axis_index("dev")
    core, chip = me % 2, me // 2
    res_copy = pltpu.make_async_copy(res_hbm, res_ref, res_sem)
    res_copy.start()
    spans, span = 8, width // 8
    per = span // 128
    sums = jnp.zeros((total, 4 * units), F32)
    squares = jnp.zeros((total, 128), F32)
    half = rows // 2
    low = lax.broadcasted_iota(jnp.int32, (groups, half, 128), 2) < 64
    lane = lax.broadcasted_iota(jnp.int32, (1, 128), 1)

    def ahead(tiles, shift):
        moved = [pltpu.roll(t, 128 - shift, 1) for t in tiles]
        return [jnp.where(lane < 128 - shift, a, b) for a, b in zip(moved, moved[1:] + moved[-1:])]

    def inverse(b):
        start = 7 * (b // 2) + 3 * (b % 2)
        tiles = [gain_ref[start + i : start + i + 1, :] for i in range(4)]
        if b % 2:
            tiles = ahead(tiles, 64)
        first, last = tiles[:2], ahead(tiles[1:], cols - 128)[:2]
        own = [jnp.where(core == 0, p, q) for p, q in zip(first, last)]
        oth = [jnp.where(core == 0, q, p) for p, q in zip(first, last)]
        third = jnp.where(lane < cols - 128, own[1], pltpu.roll(oth[1], cols - 128, 1))
        return [1.0 / own[0], 1.0 / oth[0], 1.0 / third], pltpu.roll(oth[1], 128 - (256 - cols), 1)

    for q in range(parts):

        def weights(at, size):
            return jnp.concatenate([w[pl.ds(at, size), :] for w in (go_ref, gx_ref, uo_ref, ux_ref)], axis=1)

        tiles, stacks, inverses, rests = [], [], [], {}
        for b in range(q * quarter, (q + 1) * quarter):
            own = pl.multiple_of(2 * cols * b + cols * core, 32)
            oth = pl.multiple_of(2 * cols * b + cols * (1 - core), 32)
            tiles += [x_buf[:, b, i * rows : (i + 1) * rows, :].reshape(total, 128) for i in range(3)]
            stacks += [
                weights(own, 128),
                weights(oth, 128),
                weights(pl.multiple_of(own + 128, 32), cols - 128),
                weights(pl.multiple_of(oth + 128, 32), 256 - cols),
            ]
            inv, rests[b] = inverse(b)
            inverses += inv
        for b in range(q * quarter, (q + 1) * quarter, 2):
            first, second = (x_buf[:, b + i, 3 * rows :, :].astype(F32) for i in range(2))
            top = jnp.where(low, first, second)
            bottom = jnp.where(low, second, first)
            bottom = pltpu.roll(bottom.reshape(groups * half, 128), 64, 1).reshape(groups, half, 128)
            tiles.append(jnp.concatenate([top, bottom], axis=1).reshape(total, 128).astype(BF16))
            inverses.append(1.0 / jnp.where(lane < 64, rests[b], pltpu.roll(rests[b + 1], 64, 1)))
            for i in range(2):
                oth = pl.multiple_of(2 * cols * (b + i) + cols * (1 - core) + (384 - cols), 32)
                stacks.append(weights(oth, 2 * cols - 384))
        x = jnp.concatenate(tiles, axis=1)
        sums += jnp.dot(x, jnp.concatenate(stacks, axis=0), preferred_element_type=F32)
        for tile, inv in zip(tiles, inverses):
            res = tile.astype(F32) * inv
            squares += res * res

    scale = lax.rsqrt(jnp.sum(squares, axis=1, keepdims=True) / width + EPS)
    gate = sums[:, : 2 * units] * scale
    up = sums[:, 2 * units :] * scale
    act = (gate / (1.0 + jnp.exp(-gate)) * up).astype(BF16)

    for b in range(spans):
        some = slice(b * span, (b + 1) * span)
        w = jnp.concatenate([do_ref[some, :], dx_ref[some, :]], axis=1)
        product = lax.dot_general(act, w, NT, preferred_element_type=F32).astype(BF16)
        for t in range(per):
            held[b * per + t] = product[:, t * 128 : (t + 1) * 128]
    res_copy.wait()
    mine = pl.multiple_of(rows * lax.axis_index("grp"), rows)
    start = 7 * (chip // 2) + 3 * (chip % 2)
    for i in range(4):
        at = (pl.ds(start + i, 1), pl.ds(mine, rows))
        held[at] = (held[at].astype(F32) + res_ref[i : i + 1]).astype(BF16)

    r = lax.broadcasted_iota(jnp.int32, (128, 128), 0)
    c = lax.broadcasted_iota(jnp.int32, (128, 128), 1)
    peer, piece, slot = r // 16, (r // 2) % spans, r % 2
    order = jnp.where(c == piece * 16 + peer * 2 + slot, 1.0, 0.0).astype(BF16)
    outs = []
    for g in range(total // 16):
        stack = jnp.concatenate(
            [
                jnp.concatenate([held[b * per + t, g * 16 : (g + 1) * 16, :] for t in range(per)], axis=1)
                for b in range(spans)
            ],
            axis=0,
        )
        moved = jnp.dot(order, stack, preferred_element_type=F32).astype(BF16)
        some = pl.ds(g * 8, 8)
        out_buf[g * 8 : (g + 1) * 8] = moved.reshape(8, 16, span)
        outs.append(pltpu.make_async_copy(out_buf.at[some], out_hbm.at[some], out_sem.at[g]))
        outs[-1].start()
    for out in outs:
        out.wait()


def feed_forward(blocks, gate, up, down, gain, residual, chips):
    peers, packed, _ = blocks.shape
    groups = peers // chips
    width, units = gate[0].shape
    cols = width // chips // 2
    rows = packed * 128 // (2 * cols)
    total = groups * rows
    spans = 8
    span = width // spans
    vmem = pl.BlockSpec(memory_space=pltpu.VMEM)
    return pl.pallas_call(
        functools.partial(ffn_kernel, chips, cols, width),
        in_specs=[vmem] * 8 + [pl.BlockSpec(memory_space=pl.ANY)],
        out_specs=pl.BlockSpec(memory_space=pl.ANY),
        out_shape=pltpu.HBM((peers, 16, span), BF16),
        scratch_shapes=[
            pltpu.VMEM((width // 128, total, 128), BF16),
            pltpu.VMEM((peers, 16, span), BF16),
            pltpu.VMEM(residual.shape, F32),
            pltpu.SemaphoreType.DMA,
            pltpu.SemaphoreType.DMA((total // 16,)),
        ],
        compiler_params=pltpu.CompilerParams(vmem_limit_bytes=28 * 2**20),
        cost_estimate=pl.CostEstimate(
            flops=12 * total * units * width, bytes_accessed=14 * width * units, transcendentals=0
        ),
    )(
        blocks.reshape(groups, chips, packed, 128),
        *gate,
        *up,
        *down,
        gain,
        in_hbm(residual),
    )


def final_kernel(lengths_ref, parts_ref, out_ref):
    total = jnp.zeros(parts_ref.shape[1:], F32)
    for p in range(parts_ref.shape[0]):
        total += parts_ref[p].astype(F32)
    row = lax.broadcasted_iota(jnp.int32, total.shape, 0)
    live = jnp.where(row % 2 == 0, lengths_ref[0], lengths_ref[1]) > 0
    total = jnp.where(live, total, 0.0)
    span = total.shape[1]
    for b in range(total.shape[0] // 2):
        out_ref[:, b * span : (b + 1) * span] = total[2 * b : 2 * b + 2].astype(BF16)


def finish(lengths, parts):
    _, rows, span = parts.shape
    return pl.pallas_call(
        final_kernel,
        in_specs=[pl.BlockSpec(memory_space=pltpu.SMEM), pl.BlockSpec(memory_space=pltpu.VMEM)],
        out_specs=pl.BlockSpec(memory_space=pltpu.VMEM),
        out_shape=jax.ShapeDtypeStruct((2, rows * span // 2), BF16),
        compiler_params=pltpu.CompilerParams(vmem_limit_bytes=16 * 2**20),
    )(in_hbm(lengths), parts)


def make_shards(groups, devs):
    chips = devs // 2
    peers = groups * chips
    plane = [[2 * k + c for k in range(chips)] for c in range(2)]
    cube = [[2 * k + c for k in range(peers)] for c in range(2)]
    other = [(i, i ^ 1) for i in range(devs)]
    both = ("grp", "dev")
    near = [(i, i ^ 2) for i in range(1, groups * devs, 2)]
    far = [
        (x * devs + i, (x + groups // 2) % groups * devs + (i + devs // 2 + 4) % devs) for x in range(groups) for i in range(1, devs, 2)
    ]

    def shards(
        query,
        key_cache,
        value_cache,
        lengths,
        hidden,
        out_weight,
        ffn_gain,
        gate_weight,
        up_weight,
        down_weight,
    ):
        slots, width = hidden.shape

        def swap(w):
            return lax.ppermute(w, "dev", other)

        out_own = out_weight.T
        out_oth = swap(out_own)
        gate = (gate_weight, swap(gate_weight))
        up = (up_weight, swap(up_weight))
        down = (down_weight, swap(down_weight))
        token = lengths
        for link in (far, near):
            token = lax.ppermute(token, both, link)
        message = attend(lengths, query, key_cache, value_cache, hidden, token, chips)
        got = lax.all_to_all(message, "dev", 0, 0, axis_index_groups=plane)
        gain = ffn_gain.reshape(width // 128, 128)
        block, residual = project(got, gain, out_own, out_oth, (gate[1], up[1], down[1]), peers)

        blocks = lax.all_to_all(block, both, 0, 0, axis_index_groups=cube)
        partial = feed_forward(blocks, gate, up, down, gain, residual, chips)
        parts = lax.all_to_all(partial, both, 0, 0, axis_index_groups=cube)
        return finish(lengths, parts)

    return shards


def solution(mesh):
    both = ("grp", "dev")
    in_specs = (
        P(both, None),
        P(both, None, None),
        P(both, None, None),
        P(both),
        P(both, None),
        P(None, "dev"),
        P(),
        P(None, both),
        P(None, both),
        P(None, both),
    )
    body = make_shards(mesh.shape["grp"], mesh.shape["dev"])
    return jax.shard_map(body, mesh=mesh, in_specs=in_specs, out_specs=P(both, None), check_vma=False)
```

```python
import functools

import jax
import jax.numpy as jnp
from jax import lax
from jax.experimental import pallas as pl
from jax.experimental.pallas import tpu as pltpu
from jax.sharding import PartitionSpec as P

BF16 = jnp.bfloat16
F32 = jnp.float32
EPS = 1e-05
VMEM = 32 * 2**20
NT = (((1,), (1,)), ((), ()))


def attend_kernel(lengths_ref, q_hbm, k_hbm, v_hbm, hid_hbm, token_hbm, out_ref, q_ref, hid_ref, keys, values, small_sems, sems):
    slots, span, dim = keys.shape
    heads = q_ref.shape[1] // dim
    chips = out_ref.shape[0]
    small = [
        pltpu.make_async_copy(src, dst, small_sems.at[i])
        for i, (src, dst) in enumerate(((q_hbm, q_ref), (hid_hbm, hid_ref)))
    ]
    for copy in small:
        copy.start()
    copies = []
    for i, (src, dst) in enumerate(((k_hbm, keys), (v_hbm, values))):
        for s in range(slots):
            copy = pltpu.make_async_copy(src.at[s], dst.at[s], sems.at[i, s])
            copy.start()
            copies.append(copy)
    small[0].wait()
    q = q_ref[...].astype(F32)
    q = jnp.concatenate(
        [q[s : s + 1, h * dim : (h + 1) * dim] for s in range(slots) for h in range(heads)], axis=0
    ).astype(BF16)
    small[1].wait()
    hid = hid_ref[...].astype(F32)
    row = lax.broadcasted_iota(jnp.int32, (16, 128), 0)
    tiles = [
        jnp.where(row % slots == 0, hid[0:1, t * 128 : (t + 1) * 128], hid[1:2, t * 128 : (t + 1) * 128])
        for t in range(hid.shape[1] // 128)
    ]
    extra = []
    for p in range(chips):
        first = (p * hid.shape[1] // chips) // 128
        held = jnp.zeros((16, 128), F32)
        for i in range(4):
            held = jnp.where(row // slots == i, tiles[first + i], held)
        extra.append(held.astype(BF16))
    parts = []
    position = lax.broadcasted_iota(jnp.int32, (heads, span), 1)
    for copy in copies[:slots]:
        copy.wait()
    scores = [
        lax.dot_general(q[s * heads : (s + 1) * heads, :], keys[s], NT, preferred_element_type=F32)
        for s in range(slots)
    ]
    for copy in copies[slots:]:
        copy.wait()
    for s in range(slots):
        score = jnp.where(position < jnp.maximum(lengths_ref[s], 1), scores[s] * dim ** (-0.5), -jnp.inf)
        weights = jnp.exp(score - jnp.max(score, axis=1, keepdims=True))
        probs = (weights * (1.0 / jnp.sum(weights, axis=1, keepdims=True))).astype(BF16)
        parts.append(jnp.dot(probs, values[s], preferred_element_type=F32).astype(BF16))
    both = jnp.concatenate(parts, axis=0)
    pieces = 16 // slots
    per = heads // pieces
    r = lax.broadcasted_iota(jnp.int32, (16, slots * heads), 0)
    c = lax.broadcasted_iota(jnp.int32, (16, slots * heads), 1)
    rows = []
    for j in range(per):
        take = jnp.where(c == (r % slots) * heads + (r // slots) * per + j, 1.0, 0.0).astype(BF16)
        rows.append(jnp.dot(take, both, preferred_element_type=F32).astype(BF16))
    rows = jnp.concatenate(rows, axis=1)
    for p in range(chips):
        out_ref[p] = jnp.concatenate([rows, extra[p]], axis=1)


def attend(lengths, query, key_cache, value_cache, hidden, token, chips):
    slots, span, dim = key_cache.shape
    hbm = pl.BlockSpec(memory_space=pl.ANY)
    vmem = pl.BlockSpec(memory_space=pltpu.VMEM)
    lanes = query.shape[1] * slots // 16 + 128
    return pl.pallas_call(
        attend_kernel,
        in_specs=[pl.BlockSpec(memory_space=pltpu.SMEM)] + [hbm] * 5,
        out_specs=vmem,
        out_shape=pltpu.HBM((chips, 16, lanes), BF16),
        scratch_shapes=[
            pltpu.VMEM(query.shape, BF16),
            pltpu.VMEM(hidden.shape, BF16),
            pltpu.VMEM(key_cache.shape, BF16),
            pltpu.VMEM(value_cache.shape, BF16),
            pltpu.SemaphoreType.DMA((2,)),
            pltpu.SemaphoreType.DMA((2, slots)),
        ],
        compiler_params=pltpu.CompilerParams(vmem_limit_bytes=12 * 2**20),
    )(in_hbm(lengths), *[in_hbm(v) for v in (query, key_cache, value_cache, hidden)], token)


def project_kernel(cols, x_ref, own, oth, gain_hbm, *refs):
    out_hbm, res_hbm, gain_ref, res_ref, block, gain_sem, res_sem, out_sem = refs[-8:]
    gain_copy = pltpu.make_async_copy(gain_hbm, gain_ref, gain_sem)
    gain_copy.start()
    chips, deep, lanes = x_ref.shape
    slots = 2
    pieces = deep // slots
    rows = chips * slots
    wide = own.shape[1] // pieces
    r = lax.broadcasted_iota(jnp.int32, (chips * deep, chips * deep), 0)
    c = lax.broadcasted_iota(jnp.int32, (chips * deep, chips * deep), 1)
    order = c == (r % rows) // slots * deep + r // rows * slots + r % slots
    order = jnp.where(order, 1.0, 0.0).astype(BF16)
    x = jnp.dot(order, x_ref[...].reshape(chips * deep, lanes), preferred_element_type=F32)
    hid_rows = [x[i * rows : (i + 1) * rows, wide:] for i in range(4)]
    x = jnp.concatenate([x[i * rows : (i + 1) * rows, :wide] for i in range(pieces)], axis=1).astype(BF16)
    sums = [lax.dot_general(x, w[...], NT, preferred_element_type=F32) for w in (own, oth)]
    me = lax.axis_index("dev")
    core, chip = me % 2, me // 2
    lane = lax.broadcasted_iota(jnp.int32, (rows, 128), 1)

    def ahead(tiles, shift):
        moved = [pltpu.roll(t, 128 - shift, 1) for t in tiles]
        return [jnp.where(lane < 128 - shift, a, b) for a, b in zip(moved, moved[1:] + moved[-1:])]

    def halves(tiles):
        tiles = [jnp.where(chip % 2 == 0, a, b) for a, b in zip(tiles, ahead(tiles, 64))]
        first = jnp.concatenate(tiles[:2], axis=1)
        second = jnp.concatenate(ahead(tiles[1:], cols - 128)[:2], axis=1)
        return jnp.where(core == 0, first, second), jnp.where(core == 0, second, first)

    hids = halves(hid_rows)
    start = 7 * (chip // 2) + 3 * (chip % 2)
    gain_copy.wait()
    gains = halves([jnp.broadcast_to(gain_ref[pl.ds(start + i, 1), :], (rows, 128)) for i in range(4)])
    pad = jnp.zeros((rows, 256 - cols), F32)
    held, sent = [], []
    for acc, hid, gain in zip(sums, hids, gains):
        projected = jnp.concatenate([acc.astype(BF16).astype(F32), pad], axis=1)
        held.append(hid + projected)
        sent.append(held[-1] * gain)

    first = jnp.where(core == 0, held[0], held[1])
    second = jnp.where(core == 0, held[1], held[0])
    near, far = pltpu.roll(second[:, :128], cols - 128, 1), pltpu.roll(second[:, 128:], cols - 128, 1)
    tiles = [
        first[:, :128],
        jnp.where(lane < cols - 128, first[:, 128:], near),
        jnp.where(lane < cols - 128, near, far),
        jnp.where(lane < 64, far, 0.0),
    ]
    moved = [pltpu.roll(t, 64, 1) for t in tiles]
    for i in range(4):
        before = moved[i - 1] if i else jnp.zeros((rows, 128), F32)
        res_ref[i] = jnp.where(chip % 2 == 0, tiles[i], jnp.where(lane < 64, before, moved[i]))
    own_tail, oth_tail = sent[0][:, 128:], sent[1][:, 128:]
    third = jnp.where(lane < cols - 128, own_tail, pltpu.roll(oth_tail, cols - 128, 1))
    rest = pltpu.roll(oth_tail, 128 - (256 - cols), 1)
    turned = pltpu.roll(rest, 64, 1)
    half = rows // 2
    low = lax.broadcasted_iota(jnp.int32, (half, 128), 1) < 64
    even = jnp.where(low, rest[:half], turned[half:])
    odd = jnp.where(low, rest[half:], turned[:half])
    last = jnp.where(chip % 2 == 0, even, odd)
    packed = jnp.concatenate([sent[0][:, :128], sent[1][:, :128], third, last], axis=0).astype(BF16)
    many = block.shape[0]
    for p in range(many):
        block[p] = packed
    outs = [pltpu.make_async_copy(res_ref, res_hbm, res_sem)]
    outs[0].start()
    for p in range(out_hbm.shape[0] // many):
        out = pltpu.make_async_copy(block, out_hbm.at[pl.ds(p * many, many)], out_sem.at[p])
        out.start()
        outs.append(out)
    for out in outs:
        out.wait()


def in_hbm(v):
    return pltpu.with_memory_space_constraint(v, pltpu.HBM)


def project(messages, gain, out_own, out_oth, arrived, peers):
    cols, depth = out_own.shape
    rows = messages.shape[0] * 2
    packed = rows * 2 * cols // 128
    hbm = pl.BlockSpec(memory_space=pl.ANY)
    return pl.pallas_call(
        functools.partial(project_kernel, cols),
        in_specs=[pl.BlockSpec(memory_space=pltpu.VMEM)] * 3 + [hbm] * (1 + len(arrived)),
        out_specs=[hbm, hbm],
        out_shape=[pltpu.HBM((peers, packed, 128), BF16), pltpu.HBM((4, rows, 128), F32)],
        scratch_shapes=[
            pltpu.VMEM(gain.shape, F32),
            pltpu.VMEM((4, rows, 128), F32),
            pltpu.VMEM((8, packed, 128), BF16),
            pltpu.SemaphoreType.DMA,
            pltpu.SemaphoreType.DMA,
            pltpu.SemaphoreType.DMA((peers // 8,)),
        ],
        compiler_params=pltpu.CompilerParams(vmem_limit_bytes=24 * 2**20),
        cost_estimate=pl.CostEstimate(
            flops=4 * rows * cols * depth, bytes_accessed=4 * cols * depth, transcendentals=0
        ),
    )(messages, out_own, out_oth, in_hbm(gain), *arrived)


def ffn_kernel(
    chips, cols, width,
    x_buf, go_ref, gx_ref, uo_ref, ux_ref, do_ref, dx_ref, gain_ref, res_hbm, out_hbm,
    held, out_buf, res_ref, res_sem, out_sem,
):
    groups, _, packed, _ = x_buf.shape
    rows = packed * 128 // (2 * cols)
    total = groups * rows
    units = go_ref.shape[1]
    quarter = 4
    parts = chips // quarter
    me = lax.axis_index("dev")
    core, chip = me % 2, me // 2
    res_copy = pltpu.make_async_copy(res_hbm, res_ref, res_sem)
    res_copy.start()
    spans, span = 8, width // 8
    per = span // 128
    sums = jnp.zeros((total, 4 * units), F32)
    squares = jnp.zeros((total, 128), F32)
    half = rows // 2
    low = lax.broadcasted_iota(jnp.int32, (groups, half, 128), 2) < 64
    lane = lax.broadcasted_iota(jnp.int32, (1, 128), 1)

    def ahead(tiles, shift):
        moved = [pltpu.roll(t, 128 - shift, 1) for t in tiles]
        return [jnp.where(lane < 128 - shift, a, b) for a, b in zip(moved, moved[1:] + moved[-1:])]

    def inverse(b):
        start = 7 * (b // 2) + 3 * (b % 2)
        tiles = [gain_ref[start + i : start + i + 1, :] for i in range(4)]
        if b % 2:
            tiles = ahead(tiles, 64)
        first, last = tiles[:2], ahead(tiles[1:], cols - 128)[:2]
        own = [jnp.where(core == 0, p, q) for p, q in zip(first, last)]
        oth = [jnp.where(core == 0, q, p) for p, q in zip(first, last)]
        third = jnp.where(lane < cols - 128, own[1], pltpu.roll(oth[1], cols - 128, 1))
        return [1.0 / own[0], 1.0 / oth[0], 1.0 / third], pltpu.roll(oth[1], 128 - (256 - cols), 1)

    for q in range(parts):

        def weights(at, size):
            return jnp.concatenate([w[pl.ds(at, size), :] for w in (go_ref, gx_ref, uo_ref, ux_ref)], axis=1)

        tiles, stacks, inverses, rests = [], [], [], {}
        for b in range(q * quarter, (q + 1) * quarter):
            own = pl.multiple_of(2 * cols * b + cols * core, 32)
            oth = pl.multiple_of(2 * cols * b + cols * (1 - core), 32)
            tiles += [x_buf[:, b, i * rows : (i + 1) * rows, :].reshape(total, 128) for i in range(3)]
            stacks += [
                weights(own, 128),
                weights(oth, 128),
                weights(pl.multiple_of(own + 128, 32), cols - 128),
                weights(pl.multiple_of(oth + 128, 32), 256 - cols),
            ]
            inv, rests[b] = inverse(b)
            inverses += inv
        for b in range(q * quarter, (q + 1) * quarter, 2):
            first, second = (x_buf[:, b + i, 3 * rows :, :].astype(F32) for i in range(2))
            top = jnp.where(low, first, second)
            bottom = jnp.where(low, second, first)
            bottom = pltpu.roll(bottom.reshape(groups * half, 128), 64, 1).reshape(groups, half, 128)
            tiles.append(jnp.concatenate([top, bottom], axis=1).reshape(total, 128).astype(BF16))
            inverses.append(1.0 / jnp.where(lane < 64, rests[b], pltpu.roll(rests[b + 1], 64, 1)))
            for i in range(2):
                oth = pl.multiple_of(2 * cols * (b + i) + cols * (1 - core) + (384 - cols), 32)
                stacks.append(weights(oth, 2 * cols - 384))
        x = jnp.concatenate(tiles, axis=1)
        sums += jnp.dot(x, jnp.concatenate(stacks, axis=0), preferred_element_type=F32)
        for tile, inv in zip(tiles, inverses):
            res = tile.astype(F32) * inv
            squares += res * res

    res_copy.wait()
    scale = lax.rsqrt(jnp.sum(squares, axis=1, keepdims=True) / width + EPS)
    gate = sums[:, : 2 * units] * scale
    up = sums[:, 2 * units :] * scale
    act = (gate / (1.0 + jnp.exp(-gate)) * up).astype(BF16)

    for b in range(spans):
        some = slice(b * span, (b + 1) * span)
        w = jnp.concatenate([do_ref[some, :], dx_ref[some, :]], axis=1)
        product = lax.dot_general(act, w, NT, preferred_element_type=F32).astype(BF16)
        for t in range(per):
            held[b * per + t] = product[:, t * 128 : (t + 1) * 128]
    mine = pl.multiple_of(rows * lax.axis_index("grp"), rows)
    start = 7 * (chip // 2) + 3 * (chip % 2)
    for i in range(4):
        at = (pl.ds(start + i, 1), pl.ds(mine, rows))
        held[at] = (held[at].astype(F32) + res_ref[i : i + 1]).astype(BF16)

    r = lax.broadcasted_iota(jnp.int32, (128, 128), 0)
    c = lax.broadcasted_iota(jnp.int32, (128, 128), 1)
    peer, piece, slot = r // 16, (r // 2) % spans, r % 2
    order = jnp.where(c == piece * 16 + peer * 2 + slot, 1.0, 0.0).astype(BF16)
    outs = []
    for g in range(total // 16):
        stack = jnp.concatenate(
            [
                jnp.concatenate([held[b * per + t, g * 16 : (g + 1) * 16, :] for t in range(per)], axis=1)
                for b in range(spans)
            ],
            axis=0,
        )
        moved = jnp.dot(order, stack, preferred_element_type=F32).astype(BF16)
        some = pl.ds(g * 8, 8)
        out_buf[g * 8 : (g + 1) * 8] = moved.reshape(8, 16, span)
        outs.append(pltpu.make_async_copy(out_buf.at[some], out_hbm.at[some], out_sem.at[g]))
        outs[-1].start()
    for out in outs:
        out.wait()


def feed_forward(blocks, gate, up, down, gain, residual, chips):
    peers, packed, _ = blocks.shape
    groups = peers // chips
    width, units = gate[0].shape
    cols = width // chips // 2
    rows = packed * 128 // (2 * cols)
    total = groups * rows
    spans = 8
    span = width // spans
    vmem = pl.BlockSpec(memory_space=pltpu.VMEM)
    return pl.pallas_call(
        functools.partial(ffn_kernel, chips, cols, width),
        in_specs=[vmem] * 8 + [pl.BlockSpec(memory_space=pl.ANY)],
        out_specs=pl.BlockSpec(memory_space=pl.ANY),
        out_shape=pltpu.HBM((peers, 16, span), BF16),
        scratch_shapes=[
            pltpu.VMEM((width // 128, total, 128), BF16),
            pltpu.VMEM((peers, 16, span), BF16),
            pltpu.VMEM(residual.shape, F32),
            pltpu.SemaphoreType.DMA,
            pltpu.SemaphoreType.DMA((total // 16,)),
        ],
        compiler_params=pltpu.CompilerParams(vmem_limit_bytes=28 * 2**20),
        cost_estimate=pl.CostEstimate(
            flops=12 * total * units * width, bytes_accessed=14 * width * units, transcendentals=0
        ),
    )(
        blocks.reshape(groups, chips, packed, 128),
        *gate,
        *up,
        *down,
        gain,
        in_hbm(residual),
    )


def final_kernel(lengths_ref, parts_ref, out_ref):
    total = jnp.zeros(parts_ref.shape[1:], F32)
    for p in range(parts_ref.shape[0]):
        total += parts_ref[p].astype(F32)
    row = lax.broadcasted_iota(jnp.int32, total.shape, 0)
    live = jnp.where(row % 2 == 0, lengths_ref[0], lengths_ref[1]) > 0
    total = jnp.where(live, total, 0.0)
    span = total.shape[1]
    for b in range(total.shape[0] // 2):
        out_ref[:, b * span : (b + 1) * span] = total[2 * b : 2 * b + 2].astype(BF16)


def finish(lengths, parts):
    _, rows, span = parts.shape
    return pl.pallas_call(
        final_kernel,
        in_specs=[pl.BlockSpec(memory_space=pltpu.SMEM), pl.BlockSpec(memory_space=pltpu.VMEM)],
        out_specs=pl.BlockSpec(memory_space=pltpu.VMEM),
        out_shape=jax.ShapeDtypeStruct((2, rows * span // 2), BF16),
        compiler_params=pltpu.CompilerParams(vmem_limit_bytes=16 * 2**20),
    )(in_hbm(lengths), parts)


def make_shards(groups, devs):
    chips = devs // 2
    peers = groups * chips
    plane = [[2 * k + c for k in range(chips)] for c in range(2)]
    cube = [[2 * k + c for k in range(peers)] for c in range(2)]
    other = [(i, i ^ 1) for i in range(devs)]
    both = ("grp", "dev")
    near = [(i, i ^ 2) for i in range(1, groups * devs, 2)]
    far = [
        (x * devs + i, (x + groups // 2) % groups * devs + (i + devs // 2 + 4) % devs) for x in range(groups) for i in range(1, devs, 2)
    ]

    def shards(
        query,
        key_cache,
        value_cache,
        lengths,
        hidden,
        out_weight,
        ffn_gain,
        gate_weight,
        up_weight,
        down_weight,
    ):
        slots, width = hidden.shape

        def swap(w):
            return lax.ppermute(w, "dev", other)

        out_own = out_weight.T
        out_oth = swap(out_own)
        gate = (gate_weight, swap(gate_weight))
        up = (up_weight, swap(up_weight))
        down = (down_weight, swap(down_weight))
        token = lengths
        for link in (far, near):
            token = lax.ppermute(token, both, link)
        message = attend(lengths, query, key_cache, value_cache, hidden, token, chips)
        got = lax.all_to_all(message, "dev", 0, 0, axis_index_groups=plane)
        gain = ffn_gain.reshape(width // 128, 128)
        block, residual = project(got, gain, out_own, out_oth, (gate[1], up[1], down[1]), peers)

        blocks = lax.all_to_all(block, both, 0, 0, axis_index_groups=cube)
        partial = feed_forward(blocks, gate, up, down, gain, residual, chips)
        parts = lax.all_to_all(partial, both, 0, 0, axis_index_groups=cube)
        return finish(lengths, parts)

    return shards


def solution(mesh):
    both = ("grp", "dev")
    in_specs = (
        P(both, None),
        P(both, None, None),
        P(both, None, None),
        P(both),
        P(both, None),
        P(None, "dev"),
        P(),
        P(None, both),
        P(None, both),
        P(None, both),
    )
    body = make_shards(mesh.shape["grp"], mesh.shape["dev"])
    return jax.shard_map(body, mesh=mesh, in_specs=in_specs, out_specs=P(both, None), check_vma=False)
```

```python
import functools

import jax
import jax.numpy as jnp
from jax import lax
from jax.experimental import pallas as pl
from jax.experimental.pallas import tpu as pltpu
from jax.sharding import PartitionSpec as P

BF16 = jnp.bfloat16
F32 = jnp.float32
EPS = 1e-05
VMEM = 32 * 2**20
NT = (((1,), (1,)), ((), ()))


def attend_kernel(lengths_ref, q_hbm, k_hbm, v_hbm, hid_hbm, token_hbm, out_ref, q_ref, hid_ref, keys, values, small_sems, sems):
    slots, span, dim = keys.shape
    heads = q_ref.shape[1] // dim
    chips = out_ref.shape[0]
    small = [
        pltpu.make_async_copy(src, dst, small_sems.at[i])
        for i, (src, dst) in enumerate(((q_hbm, q_ref), (hid_hbm, hid_ref)))
    ]
    for copy in small:
        copy.start()
    copies = []
    for i, (src, dst) in enumerate(((k_hbm, keys), (v_hbm, values))):
        for s in range(slots):
            copy = pltpu.make_async_copy(src.at[s], dst.at[s], sems.at[i, s])
            copy.start()
            copies.append(copy)
    small[0].wait()
    q = q_ref[...].astype(F32)
    q = jnp.concatenate(
        [q[s : s + 1, h * dim : (h + 1) * dim] for s in range(slots) for h in range(heads)], axis=0
    ).astype(BF16)
    small[1].wait()
    hid = hid_ref[...].astype(F32)
    row = lax.broadcasted_iota(jnp.int32, (16, 128), 0)
    tiles = [
        jnp.where(row % slots == 0, hid[0:1, t * 128 : (t + 1) * 128], hid[1:2, t * 128 : (t + 1) * 128])
        for t in range(hid.shape[1] // 128)
    ]
    extra = []
    for p in range(chips):
        first = (p * hid.shape[1] // chips) // 128
        held = jnp.zeros((16, 128), F32)
        for i in range(4):
            held = jnp.where(row // slots == i, tiles[first + i], held)
        extra.append(held.astype(BF16))
    parts = []
    position = lax.broadcasted_iota(jnp.int32, (heads, span), 1)
    for copy in copies[:slots]:
        copy.wait()
    scores = [
        lax.dot_general(q[s * heads : (s + 1) * heads, :], keys[s], NT, preferred_element_type=F32)
        for s in range(slots)
    ]
    for copy in copies[slots:]:
        copy.wait()
    for s in range(slots):
        score = jnp.where(position < jnp.maximum(lengths_ref[s], 1), scores[s] * dim ** (-0.5), -jnp.inf)
        weights = jnp.exp(score - jnp.max(score, axis=1, keepdims=True))
        probs = (weights * (1.0 / jnp.sum(weights, axis=1, keepdims=True))).astype(BF16)
        parts.append(jnp.dot(probs, values[s], preferred_element_type=F32).astype(BF16))
    both = jnp.concatenate(parts, axis=0)
    pieces = 16 // slots
    per = heads // pieces
    r = lax.broadcasted_iota(jnp.int32, (16, slots * heads), 0)
    c = lax.broadcasted_iota(jnp.int32, (16, slots * heads), 1)
    rows = []
    for j in range(per):
        take = jnp.where(c == (r % slots) * heads + (r // slots) * per + j, 1.0, 0.0).astype(BF16)
        rows.append(jnp.dot(take, both, preferred_element_type=F32).astype(BF16))
    rows = jnp.concatenate(rows, axis=1)
    for p in range(chips):
        out_ref[p] = jnp.concatenate([rows, extra[p]], axis=1)


def attend(lengths, query, key_cache, value_cache, hidden, token, chips):
    slots, span, dim = key_cache.shape
    hbm = pl.BlockSpec(memory_space=pl.ANY)
    vmem = pl.BlockSpec(memory_space=pltpu.VMEM)
    lanes = query.shape[1] * slots // 16 + 128
    return pl.pallas_call(
        attend_kernel,
        in_specs=[pl.BlockSpec(memory_space=pltpu.SMEM)] + [hbm] * 5,
        out_specs=vmem,
        out_shape=jax.ShapeDtypeStruct((chips, 16, lanes), BF16),
        scratch_shapes=[
            pltpu.VMEM(query.shape, BF16),
            pltpu.VMEM(hidden.shape, BF16),
            pltpu.VMEM(key_cache.shape, BF16),
            pltpu.VMEM(value_cache.shape, BF16),
            pltpu.SemaphoreType.DMA((2,)),
            pltpu.SemaphoreType.DMA((2, slots)),
        ],
        compiler_params=pltpu.CompilerParams(vmem_limit_bytes=12 * 2**20),
    )(in_hbm(lengths), *[in_hbm(v) for v in (query, key_cache, value_cache, hidden)], token)


def project_kernel(cols, x_ref, own, oth, gain_hbm, *refs):
    out_ref, res_ref, gain_ref, gain_sem = refs[-4:]
    gain_copy = pltpu.make_async_copy(gain_hbm, gain_ref, gain_sem)
    gain_copy.start()
    chips, deep, lanes = x_ref.shape
    slots = 2
    pieces = deep // slots
    rows = chips * slots
    wide = own.shape[1] // pieces
    r = lax.broadcasted_iota(jnp.int32, (chips * deep, chips * deep), 0)
    c = lax.broadcasted_iota(jnp.int32, (chips * deep, chips * deep), 1)
    order = c == (r % rows) // slots * deep + r // rows * slots + r % slots
    order = jnp.where(order, 1.0, 0.0).astype(BF16)
    x = jnp.dot(order, x_ref[...].reshape(chips * deep, lanes), preferred_element_type=F32)
    hid_rows = [x[i * rows : (i + 1) * rows, wide:] for i in range(4)]
    x = jnp.concatenate([x[i * rows : (i + 1) * rows, :wide] for i in range(pieces)], axis=1).astype(BF16)
    sums = [lax.dot_general(x, w[...], NT, preferred_element_type=F32) for w in (own, oth)]
    me = lax.axis_index("dev")
    core, chip = me % 2, me // 2
    lane = lax.broadcasted_iota(jnp.int32, (rows, 128), 1)

    def ahead(tiles, shift):
        moved = [pltpu.roll(t, 128 - shift, 1) for t in tiles]
        return [jnp.where(lane < 128 - shift, a, b) for a, b in zip(moved, moved[1:] + moved[-1:])]

    def halves(tiles):
        tiles = [jnp.where(chip % 2 == 0, a, b) for a, b in zip(tiles, ahead(tiles, 64))]
        first = jnp.concatenate(tiles[:2], axis=1)
        second = jnp.concatenate(ahead(tiles[1:], cols - 128)[:2], axis=1)
        return jnp.where(core == 0, first, second), jnp.where(core == 0, second, first)

    hids = halves(hid_rows)
    start = 7 * (chip // 2) + 3 * (chip % 2)
    gain_copy.wait()
    gains = halves([jnp.broadcast_to(gain_ref[pl.ds(start + i, 1), :], (rows, 128)) for i in range(4)])
    pad = jnp.zeros((rows, 256 - cols), F32)
    held, sent = [], []
    for acc, hid, gain in zip(sums, hids, gains):
        projected = jnp.concatenate([acc.astype(BF16).astype(F32), pad], axis=1)
        held.append(hid + projected)
        sent.append(held[-1] * gain)

    first = jnp.where(core == 0, held[0], held[1])
    second = jnp.where(core == 0, held[1], held[0])
    near, far = pltpu.roll(second[:, :128], cols - 128, 1), pltpu.roll(second[:, 128:], cols - 128, 1)
    tiles = [
        first[:, :128],
        jnp.where(lane < cols - 128, first[:, 128:], near),
        jnp.where(lane < cols - 128, near, far),
        jnp.where(lane < 64, far, 0.0),
    ]
    moved = [pltpu.roll(t, 64, 1) for t in tiles]
    for i in range(4):
        before = moved[i - 1] if i else jnp.zeros((rows, 128), F32)
        res_ref[i] = jnp.where(chip % 2 == 0, tiles[i], jnp.where(lane < 64, before, moved[i]))
    own_tail, oth_tail = sent[0][:, 128:], sent[1][:, 128:]
    third = jnp.where(lane < cols - 128, own_tail, pltpu.roll(oth_tail, cols - 128, 1))
    rest = pltpu.roll(oth_tail, 128 - (256 - cols), 1)
    turned = pltpu.roll(rest, 64, 1)
    half = rows // 2
    low = lax.broadcasted_iota(jnp.int32, (half, 128), 1) < 64
    even = jnp.where(low, rest[:half], turned[half:])
    odd = jnp.where(low, rest[half:], turned[:half])
    last = jnp.where(chip % 2 == 0, even, odd)
    packed = jnp.concatenate([sent[0][:, :128], sent[1][:, :128], third, last], axis=0).astype(BF16)
    for p in range(out_ref.shape[0]):
        out_ref[p] = packed


def in_hbm(v):
    return pltpu.with_memory_space_constraint(v, pltpu.HBM)


def project(messages, gain, out_own, out_oth, arrived, peers):
    cols, depth = out_own.shape
    rows = messages.shape[0] * 2
    packed = rows * 2 * cols // 128
    hbm = pl.BlockSpec(memory_space=pl.ANY)
    return pl.pallas_call(
        functools.partial(project_kernel, cols),
        in_specs=[pl.BlockSpec(memory_space=pltpu.VMEM)] * 3 + [hbm] * (1 + len(arrived)),
        out_specs=[pl.BlockSpec(memory_space=pltpu.VMEM)] * 2,
        out_shape=[
            jax.ShapeDtypeStruct((peers, packed, 128), BF16),
            jax.ShapeDtypeStruct((4, rows, 128), F32),
        ],
        scratch_shapes=[
            pltpu.VMEM(gain.shape, F32),
            pltpu.SemaphoreType.DMA,
        ],
        compiler_params=pltpu.CompilerParams(vmem_limit_bytes=24 * 2**20),
        cost_estimate=pl.CostEstimate(
            flops=4 * rows * cols * depth, bytes_accessed=4 * cols * depth, transcendentals=0
        ),
    )(messages, out_own, out_oth, in_hbm(gain), *arrived)


def ffn_kernel(
    chips, cols, width,
    x_buf, go_ref, gx_ref, uo_ref, ux_ref, do_ref, dx_ref, gain_ref, res_ref, out_ref, held,
):
    groups, _, packed, _ = x_buf.shape
    rows = packed * 128 // (2 * cols)
    total = groups * rows
    units = go_ref.shape[1]
    quarter = 4
    parts = chips // quarter
    me = lax.axis_index("dev")
    core, chip = me % 2, me // 2
    spans, span = 8, width // 8
    per = span // 128
    sums = jnp.zeros((total, 4 * units), F32)
    squares = jnp.zeros((total, 128), F32)
    half = rows // 2
    low = lax.broadcasted_iota(jnp.int32, (groups, half, 128), 2) < 64
    lane = lax.broadcasted_iota(jnp.int32, (1, 128), 1)

    def ahead(tiles, shift):
        moved = [pltpu.roll(t, 128 - shift, 1) for t in tiles]
        return [jnp.where(lane < 128 - shift, a, b) for a, b in zip(moved, moved[1:] + moved[-1:])]

    def inverse(b):
        start = 7 * (b // 2) + 3 * (b % 2)
        tiles = [gain_ref[start + i : start + i + 1, :] for i in range(4)]
        if b % 2:
            tiles = ahead(tiles, 64)
        first, last = tiles[:2], ahead(tiles[1:], cols - 128)[:2]
        own = [jnp.where(core == 0, p, q) for p, q in zip(first, last)]
        oth = [jnp.where(core == 0, q, p) for p, q in zip(first, last)]
        third = jnp.where(lane < cols - 128, own[1], pltpu.roll(oth[1], cols - 128, 1))
        return [1.0 / own[0], 1.0 / oth[0], 1.0 / third], pltpu.roll(oth[1], 128 - (256 - cols), 1)

    for q in range(parts):

        def weights(at, size):
            return jnp.concatenate([w[pl.ds(at, size), :] for w in (go_ref, gx_ref, uo_ref, ux_ref)], axis=1)

        tiles, stacks, inverses, rests = [], [], [], {}
        for b in range(q * quarter, (q + 1) * quarter):
            own = pl.multiple_of(2 * cols * b + cols * core, 32)
            oth = pl.multiple_of(2 * cols * b + cols * (1 - core), 32)
            tiles += [x_buf[:, b, i * rows : (i + 1) * rows, :].reshape(total, 128) for i in range(3)]
            stacks += [
                weights(own, 128),
                weights(oth, 128),
                weights(pl.multiple_of(own + 128, 32), cols - 128),
                weights(pl.multiple_of(oth + 128, 32), 256 - cols),
            ]
            inv, rests[b] = inverse(b)
            inverses += inv
        for b in range(q * quarter, (q + 1) * quarter, 2):
            first, second = (x_buf[:, b + i, 3 * rows :, :].astype(F32) for i in range(2))
            top = jnp.where(low, first, second)
            bottom = jnp.where(low, second, first)
            bottom = pltpu.roll(bottom.reshape(groups * half, 128), 64, 1).reshape(groups, half, 128)
            tiles.append(jnp.concatenate([top, bottom], axis=1).reshape(total, 128).astype(BF16))
            inverses.append(1.0 / jnp.where(lane < 64, rests[b], pltpu.roll(rests[b + 1], 64, 1)))
            for i in range(2):
                oth = pl.multiple_of(2 * cols * (b + i) + cols * (1 - core) + (384 - cols), 32)
                stacks.append(weights(oth, 2 * cols - 384))
        x = jnp.concatenate(tiles, axis=1)
        sums += jnp.dot(x, jnp.concatenate(stacks, axis=0), preferred_element_type=F32)
        for tile, inv in zip(tiles, inverses):
            res = tile.astype(F32) * inv
            squares += res * res

    scale = lax.rsqrt(jnp.sum(squares, axis=1, keepdims=True) / width + EPS)
    gate = sums[:, : 2 * units] * scale
    up = sums[:, 2 * units :] * scale
    act = (gate / (1.0 + jnp.exp(-gate)) * up).astype(BF16)

    for b in range(spans):
        some = slice(b * span, (b + 1) * span)
        w = jnp.concatenate([do_ref[some, :], dx_ref[some, :]], axis=1)
        product = lax.dot_general(act, w, NT, preferred_element_type=F32).astype(BF16)
        for t in range(per):
            held[b * per + t] = product[:, t * 128 : (t + 1) * 128]
    mine = pl.multiple_of(rows * lax.axis_index("grp"), rows)
    start = 7 * (chip // 2) + 3 * (chip % 2)
    for i in range(4):
        at = (pl.ds(start + i, 1), pl.ds(mine, rows))
        held[at] = (held[at].astype(F32) + res_ref[i : i + 1]).astype(BF16)

    r = lax.broadcasted_iota(jnp.int32, (128, 128), 0)
    c = lax.broadcasted_iota(jnp.int32, (128, 128), 1)
    peer, piece, slot = r // 16, (r // 2) % spans, r % 2
    order = jnp.where(c == piece * 16 + peer * 2 + slot, 1.0, 0.0).astype(BF16)
    for g in range(total // 16):
        stack = jnp.concatenate(
            [
                jnp.concatenate([held[b * per + t, g * 16 : (g + 1) * 16, :] for t in range(per)], axis=1)
                for b in range(spans)
            ],
            axis=0,
        )
        moved = jnp.dot(order, stack, preferred_element_type=F32).astype(BF16)
        out_ref[g * 8 : (g + 1) * 8] = moved.reshape(8, 16, span)


def feed_forward(blocks, gate, up, down, gain, residual, chips):
    peers, packed, _ = blocks.shape
    groups = peers // chips
    width, units = gate[0].shape
    cols = width // chips // 2
    rows = packed * 128 // (2 * cols)
    total = groups * rows
    spans = 8
    span = width // spans
    vmem = pl.BlockSpec(memory_space=pltpu.VMEM)
    return pl.pallas_call(
        functools.partial(ffn_kernel, chips, cols, width),
        in_specs=[vmem] * 9,
        out_specs=vmem,
        out_shape=jax.ShapeDtypeStruct((peers, 16, span), BF16),
        scratch_shapes=[
            pltpu.VMEM((width // 128, total, 128), BF16),
        ],
        compiler_params=pltpu.CompilerParams(vmem_limit_bytes=28 * 2**20),
        cost_estimate=pl.CostEstimate(
            flops=12 * total * units * width, bytes_accessed=14 * width * units, transcendentals=0
        ),
    )(
        blocks.reshape(groups, chips, packed, 128),
        *gate,
        *up,
        *down,
        gain,
        residual,
    )


def final_kernel(lengths_ref, parts_ref, out_ref):
    total = jnp.zeros(parts_ref.shape[1:], F32)
    for p in range(parts_ref.shape[0]):
        total += parts_ref[p].astype(F32)
    row = lax.broadcasted_iota(jnp.int32, total.shape, 0)
    live = jnp.where(row % 2 == 0, lengths_ref[0], lengths_ref[1]) > 0
    total = jnp.where(live, total, 0.0)
    span = total.shape[1]
    for b in range(total.shape[0] // 2):
        out_ref[:, b * span : (b + 1) * span] = total[2 * b : 2 * b + 2].astype(BF16)


def finish(lengths, parts):
    _, rows, span = parts.shape
    return pl.pallas_call(
        final_kernel,
        in_specs=[pl.BlockSpec(memory_space=pltpu.SMEM), pl.BlockSpec(memory_space=pltpu.VMEM)],
        out_specs=pl.BlockSpec(memory_space=pltpu.VMEM),
        out_shape=jax.ShapeDtypeStruct((2, rows * span // 2), BF16),
        compiler_params=pltpu.CompilerParams(vmem_limit_bytes=16 * 2**20),
    )(in_hbm(lengths), parts)


def make_shards(groups, devs):
    chips = devs // 2
    peers = groups * chips
    plane = [[2 * k + c for k in range(chips)] for c in range(2)]
    cube = [[2 * k + c for k in range(peers)] for c in range(2)]
    other = [(i, i ^ 1) for i in range(devs)]
    both = ("grp", "dev")
    near = [(i, i ^ 2) for i in range(1, groups * devs, 2)]
    far = [
        (x * devs + i, (x + groups // 2) % groups * devs + (i + devs // 2 + 4) % devs) for x in range(groups) for i in range(1, devs, 2)
    ]

    def shards(
        query,
        key_cache,
        value_cache,
        lengths,
        hidden,
        out_weight,
        ffn_gain,
        gate_weight,
        up_weight,
        down_weight,
    ):
        slots, width = hidden.shape

        def swap(w):
            return lax.ppermute(w, "dev", other)

        out_own = out_weight.T
        out_oth = swap(out_own)
        gate = (gate_weight, swap(gate_weight))
        up = (up_weight, swap(up_weight))
        down = (down_weight, swap(down_weight))
        token = lengths
        for link in (far, near):
            token = lax.ppermute(token, both, link)
        message = attend(lengths, query, key_cache, value_cache, hidden, token, chips)
        got = lax.all_to_all(message, "dev", 0, 0, axis_index_groups=plane)
        gain = ffn_gain.reshape(width // 128, 128)
        block, residual = project(got, gain, out_own, out_oth, (gate[1], up[1], down[1]), peers)

        blocks = lax.all_to_all(block, both, 0, 0, axis_index_groups=cube)
        partial = feed_forward(blocks, gate, up, down, gain, residual, chips)
        parts = lax.all_to_all(partial, both, 0, 0, axis_index_groups=cube)
        return finish(lengths, parts)

    return shards


def solution(mesh):
    both = ("grp", "dev")
    in_specs = (
        P(both, None),
        P(both, None, None),
        P(both, None, None),
        P(both),
        P(both, None),
        P(None, "dev"),
        P(),
        P(None, both),
        P(None, both),
        P(None, both),
    )
    body = make_shards(mesh.shape["grp"], mesh.shape["dev"])
    return jax.shard_map(body, mesh=mesh, in_specs=in_specs, out_specs=P(both, None), check_vma=False)
```

```python
import functools

import jax
import jax.numpy as jnp
from jax import lax
from jax.experimental import pallas as pl
from jax.experimental.pallas import tpu as pltpu
from jax.sharding import PartitionSpec as P

BF16 = jnp.bfloat16
F32 = jnp.float32
EPS = 1e-05
VMEM = 32 * 2**20
NT = (((1,), (1,)), ((), ()))


def attend_kernel(lengths_ref, q_hbm, k_hbm, v_hbm, hid_hbm, token_hbm, out_ref, q_ref, hid_ref, keys, values, small_sems, sems):
    slots, span, dim = keys.shape
    heads = q_ref.shape[1] // dim
    chips = out_ref.shape[0]
    small = [
        pltpu.make_async_copy(src, dst, small_sems.at[i])
        for i, (src, dst) in enumerate(((q_hbm, q_ref), (hid_hbm, hid_ref)))
    ]
    for copy in small:
        copy.start()
    copies = []
    for i, (src, dst) in enumerate(((k_hbm, keys), (v_hbm, values))):
        for s in range(slots):
            copy = pltpu.make_async_copy(src.at[s], dst.at[s], sems.at[i, s])
            copy.start()
            copies.append(copy)
    small[0].wait()
    q = q_ref[...].astype(F32)
    q = jnp.concatenate(
        [q[s : s + 1, h * dim : (h + 1) * dim] for s in range(slots) for h in range(heads)], axis=0
    ).astype(BF16)
    small[1].wait()
    hid = hid_ref[...].astype(F32)
    row = lax.broadcasted_iota(jnp.int32, (16, 128), 0)
    tiles = [
        jnp.where(row % slots == 0, hid[0:1, t * 128 : (t + 1) * 128], hid[1:2, t * 128 : (t + 1) * 128])
        for t in range(hid.shape[1] // 128)
    ]
    extra = []
    for p in range(chips):
        first = (p * hid.shape[1] // chips) // 128
        held = jnp.zeros((16, 128), F32)
        for i in range(4):
            held = jnp.where(row // slots == i, tiles[first + i], held)
        extra.append(held.astype(BF16))
    parts = []
    position = lax.broadcasted_iota(jnp.int32, (heads, span), 1)
    for copy in copies[:slots]:
        copy.wait()
    scores = [
        lax.dot_general(q[s * heads : (s + 1) * heads, :], keys[s], NT, preferred_element_type=F32)
        for s in range(slots)
    ]
    for copy in copies[slots:]:
        copy.wait()
    for s in range(slots):
        score = jnp.where(position < jnp.maximum(lengths_ref[s], 1), scores[s] * dim ** (-0.5), -jnp.inf)
        weights = jnp.exp(score - jnp.max(score, axis=1, keepdims=True))
        probs = (weights * (1.0 / jnp.sum(weights, axis=1, keepdims=True))).astype(BF16)
        parts.append(jnp.dot(probs, values[s], preferred_element_type=F32).astype(BF16))
    both = jnp.concatenate(parts, axis=0)
    pieces = 16 // slots
    per = heads // pieces
    r = lax.broadcasted_iota(jnp.int32, (16, slots * heads), 0)
    c = lax.broadcasted_iota(jnp.int32, (16, slots * heads), 1)
    rows = []
    for j in range(per):
        take = jnp.where(c == (r % slots) * heads + (r // slots) * per + j, 1.0, 0.0).astype(BF16)
        rows.append(jnp.dot(take, both, preferred_element_type=F32).astype(BF16))
    rows = jnp.concatenate(rows, axis=1)
    for p in range(chips):
        out_ref[p] = jnp.concatenate([rows, extra[p]], axis=1)


def attend(lengths, query, key_cache, value_cache, hidden, token, chips):
    slots, span, dim = key_cache.shape
    hbm = pl.BlockSpec(memory_space=pl.ANY)
    vmem = pl.BlockSpec(memory_space=pltpu.VMEM)
    lanes = query.shape[1] * slots // 16 + 128
    return pl.pallas_call(
        attend_kernel,
        in_specs=[pl.BlockSpec(memory_space=pltpu.SMEM)] + [hbm] * 5,
        out_specs=vmem,
        out_shape=jax.ShapeDtypeStruct((chips, 16, lanes), BF16),
        scratch_shapes=[
            pltpu.VMEM(query.shape, BF16),
            pltpu.VMEM(hidden.shape, BF16),
            pltpu.VMEM(key_cache.shape, BF16),
            pltpu.VMEM(value_cache.shape, BF16),
            pltpu.SemaphoreType.DMA((2,)),
            pltpu.SemaphoreType.DMA((2, slots)),
        ],
        compiler_params=pltpu.CompilerParams(vmem_limit_bytes=12 * 2**20),
    )(in_hbm(lengths), *[in_hbm(v) for v in (query, key_cache, value_cache, hidden)], token)


def project_kernel(cols, x_ref, own, oth, gain_ref, *refs):
    out_ref, res_ref = refs[-2:]
    chips, deep, lanes = x_ref.shape
    slots = 2
    pieces = deep // slots
    rows = chips * slots
    wide = own.shape[1] // pieces
    r = lax.broadcasted_iota(jnp.int32, (chips * deep, chips * deep), 0)
    c = lax.broadcasted_iota(jnp.int32, (chips * deep, chips * deep), 1)
    order = c == (r % rows) // slots * deep + r // rows * slots + r % slots
    order = jnp.where(order, 1.0, 0.0).astype(BF16)
    x = jnp.dot(order, x_ref[...].reshape(chips * deep, lanes), preferred_element_type=F32)
    hid_rows = [x[i * rows : (i + 1) * rows, wide:] for i in range(4)]
    x = jnp.concatenate([x[i * rows : (i + 1) * rows, :wide] for i in range(pieces)], axis=1).astype(BF16)
    sums = [lax.dot_general(x, w[...], NT, preferred_element_type=F32) for w in (own, oth)]
    me = lax.axis_index("dev")
    core, chip = me % 2, me // 2
    lane = lax.broadcasted_iota(jnp.int32, (rows, 128), 1)

    def ahead(tiles, shift):
        moved = [pltpu.roll(t, 128 - shift, 1) for t in tiles]
        return [jnp.where(lane < 128 - shift, a, b) for a, b in zip(moved, moved[1:] + moved[-1:])]

    def halves(tiles):
        tiles = [jnp.where(chip % 2 == 0, a, b) for a, b in zip(tiles, ahead(tiles, 64))]
        first = jnp.concatenate(tiles[:2], axis=1)
        second = jnp.concatenate(ahead(tiles[1:], cols - 128)[:2], axis=1)
        return jnp.where(core == 0, first, second), jnp.where(core == 0, second, first)

    hids = halves(hid_rows)
    start = 7 * (chip // 2) + 3 * (chip % 2)
    gains = halves([jnp.broadcast_to(gain_ref[pl.ds(start + i, 1), :], (rows, 128)) for i in range(4)])
    pad = jnp.zeros((rows, 256 - cols), F32)
    held, sent = [], []
    for acc, hid, gain in zip(sums, hids, gains):
        projected = jnp.concatenate([acc.astype(BF16).astype(F32), pad], axis=1)
        held.append(hid + projected)
        sent.append(held[-1] * gain)

    first = jnp.where(core == 0, held[0], held[1])
    second = jnp.where(core == 0, held[1], held[0])
    near, far = pltpu.roll(second[:, :128], cols - 128, 1), pltpu.roll(second[:, 128:], cols - 128, 1)
    tiles = [
        first[:, :128],
        jnp.where(lane < cols - 128, first[:, 128:], near),
        jnp.where(lane < cols - 128, near, far),
        jnp.where(lane < 64, far, 0.0),
    ]
    moved = [pltpu.roll(t, 64, 1) for t in tiles]
    for i in range(4):
        before = moved[i - 1] if i else jnp.zeros((rows, 128), F32)
        res_ref[i] = jnp.where(chip % 2 == 0, tiles[i], jnp.where(lane < 64, before, moved[i]))
    own_tail, oth_tail = sent[0][:, 128:], sent[1][:, 128:]
    third = jnp.where(lane < cols - 128, own_tail, pltpu.roll(oth_tail, cols - 128, 1))
    rest = pltpu.roll(oth_tail, 128 - (256 - cols), 1)
    turned = pltpu.roll(rest, 64, 1)
    half = rows // 2
    low = lax.broadcasted_iota(jnp.int32, (half, 128), 1) < 64
    even = jnp.where(low, rest[:half], turned[half:])
    odd = jnp.where(low, rest[half:], turned[:half])
    last = jnp.where(chip % 2 == 0, even, odd)
    packed = jnp.concatenate([sent[0][:, :128], sent[1][:, :128], third, last], axis=0).astype(BF16)
    for p in range(out_ref.shape[0]):
        out_ref[p] = packed


def in_hbm(v):
    return pltpu.with_memory_space_constraint(v, pltpu.HBM)


def project(messages, gain, out_own, out_oth, arrived, peers):
    cols, depth = out_own.shape
    rows = messages.shape[0] * 2
    packed = rows * 2 * cols // 128
    hbm = pl.BlockSpec(memory_space=pl.ANY)
    return pl.pallas_call(
        functools.partial(project_kernel, cols),
        in_specs=[pl.BlockSpec(memory_space=pltpu.VMEM)] * 4 + [hbm] * len(arrived),
        out_specs=[pl.BlockSpec(memory_space=pltpu.VMEM)] * 2,
        out_shape=[
            jax.ShapeDtypeStruct((peers, packed, 128), BF16),
            jax.ShapeDtypeStruct((4, rows, 128), F32),
        ],
        compiler_params=pltpu.CompilerParams(vmem_limit_bytes=24 * 2**20),
        cost_estimate=pl.CostEstimate(
            flops=4 * rows * cols * depth, bytes_accessed=4 * cols * depth, transcendentals=0
        ),
    )(messages, out_own, out_oth, gain, *arrived)


def ffn_kernel(
    chips, cols, width,
    x_buf, go_ref, gx_ref, uo_ref, ux_ref, do_ref, dx_ref, gain_ref, res_ref, out_ref, held,
):
    groups, _, packed, _ = x_buf.shape
    rows = packed * 128 // (2 * cols)
    total = groups * rows
    units = go_ref.shape[1]
    quarter = 4
    parts = chips // quarter
    me = lax.axis_index("dev")
    core, chip = me % 2, me // 2
    spans, span = 8, width // 8
    per = span // 128
    sums = jnp.zeros((total, 4 * units), F32)
    squares = jnp.zeros((total, 128), F32)
    half = rows // 2
    low = lax.broadcasted_iota(jnp.int32, (groups, half, 128), 2) < 64
    lane = lax.broadcasted_iota(jnp.int32, (1, 128), 1)

    def ahead(tiles, shift):
        moved = [pltpu.roll(t, 128 - shift, 1) for t in tiles]
        return [jnp.where(lane < 128 - shift, a, b) for a, b in zip(moved, moved[1:] + moved[-1:])]

    def inverse(b):
        start = 7 * (b // 2) + 3 * (b % 2)
        tiles = [gain_ref[start + i : start + i + 1, :] for i in range(4)]
        if b % 2:
            tiles = ahead(tiles, 64)
        first, last = tiles[:2], ahead(tiles[1:], cols - 128)[:2]
        own = [jnp.where(core == 0, p, q) for p, q in zip(first, last)]
        oth = [jnp.where(core == 0, q, p) for p, q in zip(first, last)]
        third = jnp.where(lane < cols - 128, own[1], pltpu.roll(oth[1], cols - 128, 1))
        return [1.0 / own[0], 1.0 / oth[0], 1.0 / third], pltpu.roll(oth[1], 128 - (256 - cols), 1)

    for q in range(parts):

        def weights(at, size):
            return jnp.concatenate([w[pl.ds(at, size), :] for w in (go_ref, gx_ref, uo_ref, ux_ref)], axis=1)

        tiles, stacks, inverses, rests = [], [], [], {}
        for b in range(q * quarter, (q + 1) * quarter):
            own = pl.multiple_of(2 * cols * b + cols * core, 32)
            oth = pl.multiple_of(2 * cols * b + cols * (1 - core), 32)
            tiles += [x_buf[:, b, i * rows : (i + 1) * rows, :].reshape(total, 128) for i in range(3)]
            stacks += [
                weights(own, 128),
                weights(oth, 128),
                weights(pl.multiple_of(own + 128, 32), cols - 128),
                weights(pl.multiple_of(oth + 128, 32), 256 - cols),
            ]
            inv, rests[b] = inverse(b)
            inverses += inv
        for b in range(q * quarter, (q + 1) * quarter, 2):
            first, second = (x_buf[:, b + i, 3 * rows :, :].astype(F32) for i in range(2))
            top = jnp.where(low, first, second)
            bottom = jnp.where(low, second, first)
            bottom = pltpu.roll(bottom.reshape(groups * half, 128), 64, 1).reshape(groups, half, 128)
            tiles.append(jnp.concatenate([top, bottom], axis=1).reshape(total, 128).astype(BF16))
            inverses.append(1.0 / jnp.where(lane < 64, rests[b], pltpu.roll(rests[b + 1], 64, 1)))
            for i in range(2):
                oth = pl.multiple_of(2 * cols * (b + i) + cols * (1 - core) + (384 - cols), 32)
                stacks.append(weights(oth, 2 * cols - 384))
        x = jnp.concatenate(tiles, axis=1)
        sums += jnp.dot(x, jnp.concatenate(stacks, axis=0), preferred_element_type=F32)
        for tile, inv in zip(tiles, inverses):
            res = tile.astype(F32) * inv
            squares += res * res

    scale = lax.rsqrt(jnp.sum(squares, axis=1, keepdims=True) / width + EPS)
    gate = sums[:, : 2 * units] * scale
    up = sums[:, 2 * units :] * scale
    act = (gate / (1.0 + jnp.exp(-gate)) * up).astype(BF16)

    for b in range(spans):
        some = slice(b * span, (b + 1) * span)
        w = jnp.concatenate([do_ref[some, :], dx_ref[some, :]], axis=1)
        product = lax.dot_general(act, w, NT, preferred_element_type=F32).astype(BF16)
        for t in range(per):
            held[b * per + t] = product[:, t * 128 : (t + 1) * 128]
    mine = pl.multiple_of(rows * lax.axis_index("grp"), rows)
    start = 7 * (chip // 2) + 3 * (chip % 2)
    for i in range(4):
        at = (pl.ds(start + i, 1), pl.ds(mine, rows))
        held[at] = (held[at].astype(F32) + res_ref[i : i + 1]).astype(BF16)

    r = lax.broadcasted_iota(jnp.int32, (128, 128), 0)
    c = lax.broadcasted_iota(jnp.int32, (128, 128), 1)
    peer, piece, slot = r // 16, (r // 2) % spans, r % 2
    order = jnp.where(c == piece * 16 + peer * 2 + slot, 1.0, 0.0).astype(BF16)
    for g in range(total // 16):
        stack = jnp.concatenate(
            [
                jnp.concatenate([held[b * per + t, g * 16 : (g + 1) * 16, :] for t in range(per)], axis=1)
                for b in range(spans)
            ],
            axis=0,
        )
        moved = jnp.dot(order, stack, preferred_element_type=F32).astype(BF16)
        out_ref[g * 8 : (g + 1) * 8] = moved.reshape(8, 16, span)


def feed_forward(blocks, gate, up, down, gain, residual, chips):
    peers, packed, _ = blocks.shape
    groups = peers // chips
    width, units = gate[0].shape
    cols = width // chips // 2
    rows = packed * 128 // (2 * cols)
    total = groups * rows
    spans = 8
    span = width // spans
    vmem = pl.BlockSpec(memory_space=pltpu.VMEM)
    return pl.pallas_call(
        functools.partial(ffn_kernel, chips, cols, width),
        in_specs=[vmem] * 9,
        out_specs=vmem,
        out_shape=jax.ShapeDtypeStruct((peers, 16, span), BF16),
        scratch_shapes=[
            pltpu.VMEM((width // 128, total, 128), BF16),
        ],
        compiler_params=pltpu.CompilerParams(vmem_limit_bytes=28 * 2**20),
        cost_estimate=pl.CostEstimate(
            flops=12 * total * units * width, bytes_accessed=14 * width * units, transcendentals=0
        ),
    )(
        blocks.reshape(groups, chips, packed, 128),
        *gate,
        *up,
        *down,
        gain,
        residual,
    )


def final_kernel(lengths_ref, parts_ref, out_ref):
    total = jnp.zeros(parts_ref.shape[1:], F32)
    for p in range(parts_ref.shape[0]):
        total += parts_ref[p].astype(F32)
    row = lax.broadcasted_iota(jnp.int32, total.shape, 0)
    live = jnp.where(row % 2 == 0, lengths_ref[0], lengths_ref[1]) > 0
    total = jnp.where(live, total, 0.0)
    span = total.shape[1]
    for b in range(total.shape[0] // 2):
        out_ref[:, b * span : (b + 1) * span] = total[2 * b : 2 * b + 2].astype(BF16)


def finish(lengths, parts):
    _, rows, span = parts.shape
    return pl.pallas_call(
        final_kernel,
        in_specs=[pl.BlockSpec(memory_space=pltpu.SMEM), pl.BlockSpec(memory_space=pltpu.VMEM)],
        out_specs=pl.BlockSpec(memory_space=pltpu.VMEM),
        out_shape=jax.ShapeDtypeStruct((2, rows * span // 2), BF16),
        compiler_params=pltpu.CompilerParams(vmem_limit_bytes=16 * 2**20),
    )(in_hbm(lengths), parts)


def make_shards(groups, devs):
    chips = devs // 2
    peers = groups * chips
    plane = [[2 * k + c for k in range(chips)] for c in range(2)]
    cube = [[2 * k + c for k in range(peers)] for c in range(2)]
    other = [(i, i ^ 1) for i in range(devs)]
    both = ("grp", "dev")
    near = [(i, i ^ 2) for i in range(1, groups * devs, 2)]
    far = [
        (x * devs + i, (x + groups // 2) % groups * devs + (i + devs // 2 + 4) % devs) for x in range(groups) for i in range(1, devs, 2)
    ]

    def shards(
        query,
        key_cache,
        value_cache,
        lengths,
        hidden,
        out_weight,
        ffn_gain,
        gate_weight,
        up_weight,
        down_weight,
    ):
        slots, width = hidden.shape

        def swap(w):
            return lax.ppermute(w, "dev", other)

        out_own = out_weight.T
        out_oth = swap(out_own)
        gate = (gate_weight, swap(gate_weight))
        up = (up_weight, swap(up_weight))
        down = (down_weight, swap(down_weight))
        token = lengths
        for link in (far, near):
            token = lax.ppermute(token, both, link)
        message = attend(lengths, query, key_cache, value_cache, hidden, token, chips)
        got = lax.all_to_all(message, "dev", 0, 0, axis_index_groups=plane)
        gain = ffn_gain.reshape(width // 128, 128)
        block, residual = project(got, gain, out_own, out_oth, (gate[1], up[1], down[1]), peers)

        blocks = lax.all_to_all(block, both, 0, 0, axis_index_groups=cube)
        partial = feed_forward(blocks, gate, up, down, gain, residual, chips)
        parts = lax.all_to_all(partial, both, 0, 0, axis_index_groups=cube)
        return finish(lengths, parts)

    return shards


def solution(mesh):
    both = ("grp", "dev")
    in_specs = (
        P(both, None),
        P(both, None, None),
        P(both, None, None),
        P(both),
        P(both, None),
        P(None, "dev"),
        P(),
        P(None, both),
        P(None, both),
        P(None, both),
    )
    body = make_shards(mesh.shape["grp"], mesh.shape["dev"])
    return jax.shard_map(body, mesh=mesh, in_specs=in_specs, out_specs=P(both, None), check_vma=False)
```

```python
import functools

import jax
import jax.numpy as jnp
from jax import lax
from jax.experimental import pallas as pl
from jax.experimental.pallas import tpu as pltpu
from jax.sharding import PartitionSpec as P

BF16 = jnp.bfloat16
F32 = jnp.float32
EPS = 1e-05
VMEM = 32 * 2**20
NT = (((1,), (1,)), ((), ()))


def attend_kernel(lengths_ref, q_hbm, k_hbm, v_hbm, hid_hbm, token_hbm, out_ref, q_ref, hid_ref, keys, values, small_sems, sems):
    slots, span, dim = keys.shape
    heads = q_ref.shape[1] // dim
    chips = out_ref.shape[0]
    small = [
        pltpu.make_async_copy(src, dst, small_sems.at[i])
        for i, (src, dst) in enumerate(((q_hbm, q_ref), (hid_hbm, hid_ref)))
    ]
    for copy in small:
        copy.start()
    copies = []
    for i, (src, dst) in enumerate(((k_hbm, keys), (v_hbm, values))):
        for s in range(slots):
            copy = pltpu.make_async_copy(src.at[s], dst.at[s], sems.at[i, s])
            copy.start()
            copies.append(copy)
    small[0].wait()
    q = q_ref[...].astype(F32)
    q = jnp.concatenate(
        [q[s : s + 1, h * dim : (h + 1) * dim] for s in range(slots) for h in range(heads)], axis=0
    ).astype(BF16)
    small[1].wait()
    hid = hid_ref[...].astype(F32)
    row = lax.broadcasted_iota(jnp.int32, (16, 128), 0)
    tiles = [
        jnp.where(row % slots == 0, hid[0:1, t * 128 : (t + 1) * 128], hid[1:2, t * 128 : (t + 1) * 128])
        for t in range(hid.shape[1] // 128)
    ]
    extra = []
    for p in range(chips):
        first = (p * hid.shape[1] // chips) // 128
        held = jnp.zeros((16, 128), F32)
        for i in range(4):
            held = jnp.where(row // slots == i, tiles[first + i], held)
        extra.append(held.astype(BF16))
    parts = []
    position = lax.broadcasted_iota(jnp.int32, (heads, span), 1)
    for copy in copies[:slots]:
        copy.wait()
    scores = [
        lax.dot_general(q[s * heads : (s + 1) * heads, :], keys[s], NT, preferred_element_type=F32)
        for s in range(slots)
    ]
    for copy in copies[slots:]:
        copy.wait()
    for s in range(slots):
        score = jnp.where(position < jnp.maximum(lengths_ref[s], 1), scores[s] * dim ** (-0.5), -jnp.inf)
        weights = jnp.exp(score - jnp.max(score, axis=1, keepdims=True))
        probs = (weights * (1.0 / jnp.sum(weights, axis=1, keepdims=True))).astype(BF16)
        parts.append(jnp.dot(probs, values[s], preferred_element_type=F32).astype(BF16))
    both = jnp.concatenate(parts, axis=0)
    pieces = 16 // slots
    per = heads // pieces
    r = lax.broadcasted_iota(jnp.int32, (16, slots * heads), 0)
    c = lax.broadcasted_iota(jnp.int32, (16, slots * heads), 1)
    rows = []
    for j in range(per):
        take = jnp.where(c == (r % slots) * heads + (r // slots) * per + j, 1.0, 0.0).astype(BF16)
        rows.append(jnp.dot(take, both, preferred_element_type=F32).astype(BF16))
    rows = jnp.concatenate(rows, axis=1)
    for p in range(chips):
        out_ref[p] = jnp.concatenate([rows, extra[p]], axis=1)


def attend(lengths, query, key_cache, value_cache, hidden, token, chips):
    slots, span, dim = key_cache.shape
    hbm = pl.BlockSpec(memory_space=pl.ANY)
    vmem = pl.BlockSpec(memory_space=pltpu.VMEM)
    lanes = query.shape[1] * slots // 16 + 128
    return pl.pallas_call(
        attend_kernel,
        in_specs=[pl.BlockSpec(memory_space=pltpu.SMEM)] + [hbm] * 5,
        out_specs=vmem,
        out_shape=jax.ShapeDtypeStruct((chips, 16, lanes), BF16),
        scratch_shapes=[
            pltpu.VMEM(query.shape, BF16),
            pltpu.VMEM(hidden.shape, BF16),
            pltpu.VMEM(key_cache.shape, BF16),
            pltpu.VMEM(value_cache.shape, BF16),
            pltpu.SemaphoreType.DMA((2,)),
            pltpu.SemaphoreType.DMA((2, slots)),
        ],
        compiler_params=pltpu.CompilerParams(vmem_limit_bytes=12 * 2**20),
    )(in_hbm(lengths), *[in_hbm(v) for v in (query, key_cache, value_cache, hidden)], token)


def project_kernel(cols, x_ref, own, oth, gain_ref, *refs):
    out_ref, res_ref = refs[-2:]
    chips, deep, lanes = x_ref.shape
    slots = 2
    pieces = deep // slots
    rows = chips * slots
    wide = own.shape[1] // pieces
    r = lax.broadcasted_iota(jnp.int32, (chips * deep, chips * deep), 0)
    c = lax.broadcasted_iota(jnp.int32, (chips * deep, chips * deep), 1)
    order = c == (r % rows) // slots * deep + r // rows * slots + r % slots
    order = jnp.where(order, 1.0, 0.0).astype(BF16)
    x = jnp.dot(order, x_ref[...].reshape(chips * deep, lanes), preferred_element_type=F32)
    hid_rows = [x[i * rows : (i + 1) * rows, wide:] for i in range(4)]
    x = jnp.concatenate([x[i * rows : (i + 1) * rows, :wide] for i in range(pieces)], axis=1).astype(BF16)
    wider = jnp.concatenate([own[...], oth[...]], axis=0)
    both = lax.dot_general(wider, x, NT, preferred_element_type=F32)
    sums = [both[:cols].T, both[cols:].T]
    me = lax.axis_index("dev")
    core, chip = me % 2, me // 2
    lane = lax.broadcasted_iota(jnp.int32, (rows, 128), 1)

    def ahead(tiles, shift):
        moved = [pltpu.roll(t, 128 - shift, 1) for t in tiles]
        return [jnp.where(lane < 128 - shift, a, b) for a, b in zip(moved, moved[1:] + moved[-1:])]

    def halves(tiles):
        tiles = [jnp.where(chip % 2 == 0, a, b) for a, b in zip(tiles, ahead(tiles, 64))]
        first = jnp.concatenate(tiles[:2], axis=1)
        second = jnp.concatenate(ahead(tiles[1:], cols - 128)[:2], axis=1)
        return jnp.where(core == 0, first, second), jnp.where(core == 0, second, first)

    hids = halves(hid_rows)
    start = 7 * (chip // 2) + 3 * (chip % 2)
    gains = halves([jnp.broadcast_to(gain_ref[pl.ds(start + i, 1), :], (rows, 128)) for i in range(4)])
    pad = jnp.zeros((rows, 256 - cols), F32)
    held, sent = [], []
    for acc, hid, gain in zip(sums, hids, gains):
        projected = jnp.concatenate([acc.astype(BF16).astype(F32), pad], axis=1)
        held.append(hid + projected)
        sent.append(held[-1] * gain)

    first = jnp.where(core == 0, held[0], held[1])
    second = jnp.where(core == 0, held[1], held[0])
    near, far = pltpu.roll(second[:, :128], cols - 128, 1), pltpu.roll(second[:, 128:], cols - 128, 1)
    tiles = [
        first[:, :128],
        jnp.where(lane < cols - 128, first[:, 128:], near),
        jnp.where(lane < cols - 128, near, far),
        jnp.where(lane < 64, far, 0.0),
    ]
    moved = [pltpu.roll(t, 64, 1) for t in tiles]
    for i in range(4):
        before = moved[i - 1] if i else jnp.zeros((rows, 128), F32)
        res_ref[i] = jnp.where(chip % 2 == 0, tiles[i], jnp.where(lane < 64, before, moved[i]))
    own_tail, oth_tail = sent[0][:, 128:], sent[1][:, 128:]
    third = jnp.where(lane < cols - 128, own_tail, pltpu.roll(oth_tail, cols - 128, 1))
    rest = pltpu.roll(oth_tail, 128 - (256 - cols), 1)
    turned = pltpu.roll(rest, 64, 1)
    half = rows // 2
    low = lax.broadcasted_iota(jnp.int32, (half, 128), 1) < 64
    even = jnp.where(low, rest[:half], turned[half:])
    odd = jnp.where(low, rest[half:], turned[:half])
    last = jnp.where(chip % 2 == 0, even, odd)
    packed = jnp.concatenate([sent[0][:, :128], sent[1][:, :128], third, last], axis=0).astype(BF16)
    for p in range(out_ref.shape[0]):
        out_ref[p] = packed


def in_hbm(v):
    return pltpu.with_memory_space_constraint(v, pltpu.HBM)


def project(messages, gain, out_own, out_oth, arrived, peers):
    cols, depth = out_own.shape
    rows = messages.shape[0] * 2
    packed = rows * 2 * cols // 128
    hbm = pl.BlockSpec(memory_space=pl.ANY)
    return pl.pallas_call(
        functools.partial(project_kernel, cols),
        in_specs=[pl.BlockSpec(memory_space=pltpu.VMEM)] * 4 + [hbm] * len(arrived),
        out_specs=[pl.BlockSpec(memory_space=pltpu.VMEM)] * 2,
        out_shape=[
            jax.ShapeDtypeStruct((peers, packed, 128), BF16),
            jax.ShapeDtypeStruct((4, rows, 128), F32),
        ],
        compiler_params=pltpu.CompilerParams(vmem_limit_bytes=24 * 2**20),
        cost_estimate=pl.CostEstimate(
            flops=4 * rows * cols * depth, bytes_accessed=4 * cols * depth, transcendentals=0
        ),
    )(messages, out_own, out_oth, gain, *arrived)


def ffn_kernel(
    chips, cols, width,
    x_buf, go_ref, gx_ref, uo_ref, ux_ref, do_ref, dx_ref, gain_ref, res_ref, out_ref, held,
):
    groups, _, packed, _ = x_buf.shape
    rows = packed * 128 // (2 * cols)
    total = groups * rows
    units = go_ref.shape[1]
    quarter = 4
    parts = chips // quarter
    me = lax.axis_index("dev")
    core, chip = me % 2, me // 2
    spans, span = 8, width // 8
    per = span // 128
    sums = jnp.zeros((total, 4 * units), F32)
    squares = jnp.zeros((total, 128), F32)
    half = rows // 2
    low = lax.broadcasted_iota(jnp.int32, (groups, half, 128), 2) < 64
    lane = lax.broadcasted_iota(jnp.int32, (1, 128), 1)

    def ahead(tiles, shift):
        moved = [pltpu.roll(t, 128 - shift, 1) for t in tiles]
        return [jnp.where(lane < 128 - shift, a, b) for a, b in zip(moved, moved[1:] + moved[-1:])]

    def inverse(b):
        start = 7 * (b // 2) + 3 * (b % 2)
        tiles = [gain_ref[start + i : start + i + 1, :] for i in range(4)]
        if b % 2:
            tiles = ahead(tiles, 64)
        first, last = tiles[:2], ahead(tiles[1:], cols - 128)[:2]
        own = [jnp.where(core == 0, p, q) for p, q in zip(first, last)]
        oth = [jnp.where(core == 0, q, p) for p, q in zip(first, last)]
        third = jnp.where(lane < cols - 128, own[1], pltpu.roll(oth[1], cols - 128, 1))
        return [1.0 / own[0], 1.0 / oth[0], 1.0 / third], pltpu.roll(oth[1], 128 - (256 - cols), 1)

    for q in range(parts):

        def weights(at, size):
            return jnp.concatenate([w[pl.ds(at, size), :] for w in (go_ref, gx_ref, uo_ref, ux_ref)], axis=1)

        tiles, stacks, inverses, rests = [], [], [], {}
        for b in range(q * quarter, (q + 1) * quarter):
            own = pl.multiple_of(2 * cols * b + cols * core, 32)
            oth = pl.multiple_of(2 * cols * b + cols * (1 - core), 32)
            tiles += [x_buf[:, b, i * rows : (i + 1) * rows, :].reshape(total, 128) for i in range(3)]
            stacks += [
                weights(own, 128),
                weights(oth, 128),
                weights(pl.multiple_of(own + 128, 32), cols - 128),
                weights(pl.multiple_of(oth + 128, 32), 256 - cols),
            ]
            inv, rests[b] = inverse(b)
            inverses += inv
        for b in range(q * quarter, (q + 1) * quarter, 2):
            first, second = (x_buf[:, b + i, 3 * rows :, :].astype(F32) for i in range(2))
            top = jnp.where(low, first, second)
            bottom = jnp.where(low, second, first)
            bottom = pltpu.roll(bottom.reshape(groups * half, 128), 64, 1).reshape(groups, half, 128)
            tiles.append(jnp.concatenate([top, bottom], axis=1).reshape(total, 128).astype(BF16))
            inverses.append(1.0 / jnp.where(lane < 64, rests[b], pltpu.roll(rests[b + 1], 64, 1)))
            for i in range(2):
                oth = pl.multiple_of(2 * cols * (b + i) + cols * (1 - core) + (384 - cols), 32)
                stacks.append(weights(oth, 2 * cols - 384))
        x = jnp.concatenate(tiles, axis=1)
        sums += jnp.dot(x, jnp.concatenate(stacks, axis=0), preferred_element_type=F32)
        for tile, inv in zip(tiles, inverses):
            res = tile.astype(F32) * inv
            squares += res * res

    scale = lax.rsqrt(jnp.sum(squares, axis=1, keepdims=True) / width + EPS)
    gate = sums[:, : 2 * units] * scale
    up = sums[:, 2 * units :] * scale
    act = (gate / (1.0 + jnp.exp(-gate)) * up).astype(BF16)

    for b in range(spans):
        some = slice(b * span, (b + 1) * span)
        w = jnp.concatenate([do_ref[some, :], dx_ref[some, :]], axis=1)
        product = lax.dot_general(act, w, NT, preferred_element_type=F32).astype(BF16)
        for t in range(per):
            held[b * per + t] = product[:, t * 128 : (t + 1) * 128]
    mine = pl.multiple_of(rows * lax.axis_index("grp"), rows)
    start = 7 * (chip // 2) + 3 * (chip % 2)
    for i in range(4):
        at = (pl.ds(start + i, 1), pl.ds(mine, rows))
        held[at] = (held[at].astype(F32) + res_ref[i : i + 1]).astype(BF16)

    r = lax.broadcasted_iota(jnp.int32, (128, 128), 0)
    c = lax.broadcasted_iota(jnp.int32, (128, 128), 1)
    peer, piece, slot = r // 16, (r // 2) % spans, r % 2
    order = jnp.where(c == piece * 16 + peer * 2 + slot, 1.0, 0.0).astype(BF16)
    for g in range(total // 16):
        stack = jnp.concatenate(
            [
                jnp.concatenate([held[b * per + t, g * 16 : (g + 1) * 16, :] for t in range(per)], axis=1)
                for b in range(spans)
            ],
            axis=0,
        )
        moved = jnp.dot(order, stack, preferred_element_type=F32).astype(BF16)
        out_ref[g * 8 : (g + 1) * 8] = moved.reshape(8, 16, span)


def feed_forward(blocks, gate, up, down, gain, residual, chips):
    peers, packed, _ = blocks.shape
    groups = peers // chips
    width, units = gate[0].shape
    cols = width // chips // 2
    rows = packed * 128 // (2 * cols)
    total = groups * rows
    spans = 8
    span = width // spans
    vmem = pl.BlockSpec(memory_space=pltpu.VMEM)
    return pl.pallas_call(
        functools.partial(ffn_kernel, chips, cols, width),
        in_specs=[vmem] * 9,
        out_specs=vmem,
        out_shape=jax.ShapeDtypeStruct((peers, 16, span), BF16),
        scratch_shapes=[
            pltpu.VMEM((width // 128, total, 128), BF16),
        ],
        compiler_params=pltpu.CompilerParams(vmem_limit_bytes=28 * 2**20),
        cost_estimate=pl.CostEstimate(
            flops=12 * total * units * width, bytes_accessed=14 * width * units, transcendentals=0
        ),
    )(
        blocks.reshape(groups, chips, packed, 128),
        *gate,
        *up,
        *down,
        gain,
        residual,
    )


def final_kernel(lengths_ref, parts_ref, out_ref):
    total = jnp.zeros(parts_ref.shape[1:], F32)
    for p in range(parts_ref.shape[0]):
        total += parts_ref[p].astype(F32)
    row = lax.broadcasted_iota(jnp.int32, total.shape, 0)
    live = jnp.where(row % 2 == 0, lengths_ref[0], lengths_ref[1]) > 0
    total = jnp.where(live, total, 0.0)
    span = total.shape[1]
    for b in range(total.shape[0] // 2):
        out_ref[:, b * span : (b + 1) * span] = total[2 * b : 2 * b + 2].astype(BF16)


def finish(lengths, parts):
    _, rows, span = parts.shape
    return pl.pallas_call(
        final_kernel,
        in_specs=[pl.BlockSpec(memory_space=pltpu.SMEM), pl.BlockSpec(memory_space=pltpu.VMEM)],
        out_specs=pl.BlockSpec(memory_space=pltpu.VMEM),
        out_shape=jax.ShapeDtypeStruct((2, rows * span // 2), BF16),
        compiler_params=pltpu.CompilerParams(vmem_limit_bytes=16 * 2**20),
    )(in_hbm(lengths), parts)


def make_shards(groups, devs):
    chips = devs // 2
    peers = groups * chips
    plane = [[2 * k + c for k in range(chips)] for c in range(2)]
    cube = [[2 * k + c for k in range(peers)] for c in range(2)]
    other = [(i, i ^ 1) for i in range(devs)]
    both = ("grp", "dev")
    near = [(i, i ^ 2) for i in range(1, groups * devs, 2)]
    far = [
        (x * devs + i, (x + groups // 2) % groups * devs + (i + devs // 2 + 4) % devs) for x in range(groups) for i in range(1, devs, 2)
    ]

    def shards(
        query,
        key_cache,
        value_cache,
        lengths,
        hidden,
        out_weight,
        ffn_gain,
        gate_weight,
        up_weight,
        down_weight,
    ):
        slots, width = hidden.shape

        def swap(w):
            return lax.ppermute(w, "dev", other)

        out_own = out_weight.T
        out_oth = swap(out_own)
        gate = (gate_weight, swap(gate_weight))
        up = (up_weight, swap(up_weight))
        down = (down_weight, swap(down_weight))
        token = lengths
        for link in (near, far):
            token = lax.ppermute(token, both, link)
        message = attend(lengths, query, key_cache, value_cache, hidden, token, chips)
        got = lax.all_to_all(message, "dev", 0, 0, axis_index_groups=plane)
        gain = ffn_gain.reshape(width // 128, 128)
        block, residual = project(got, gain, out_own, out_oth, (gate[1], up[1], down[1]), peers)

        blocks = lax.all_to_all(block, both, 0, 0, axis_index_groups=cube)
        partial = feed_forward(blocks, gate, up, down, gain, residual, chips)
        parts = lax.all_to_all(partial, both, 0, 0, axis_index_groups=cube)
        return finish(lengths, parts)

    return shards


def solution(mesh):
    both = ("grp", "dev")
    in_specs = (
        P(both, None),
        P(both, None, None),
        P(both, None, None),
        P(both),
        P(both, None),
        P(None, "dev"),
        P(),
        P(None, both),
        P(None, both),
        P(None, both),
    )
    body = make_shards(mesh.shape["grp"], mesh.shape["dev"])
    return jax.shard_map(body, mesh=mesh, in_specs=in_specs, out_specs=P(both, None), check_vma=False)
```
